128 devices in a mesh: bx: 8 (over y_hi, z), by: 16 (over y_lo, x, core).
Axes of the slice: x: 4, y: 4 (y_hi: 2, y_lo: 2; y = y_hi * 2 + y_lo), z: 4, core: 2. Of those that a mesh axis runs over, the one named last changes fastest.
Arguments:
- excitation: bfloat16 [64, 128, 32, 128], P('bx', 'by'), may hold values from -6 to 6
- area: bfloat16 [64, 128, 128], P('bx', 'by'), may hold values from 1 to 8
- conductor: int32 [64, 128, 128], P('bx', 'by'), may hold values from 0 to 31
- near_blocks: bfloat16 [64, 128, 9, 128, 128], P('bx', 'by'), may hold values from -0.1875 to 0.1875
- near_mask: int32 [64, 128, 9], P('bx', 'by'), may hold values 0 or 1
- source_moments: bfloat16 [64, 128, 128, 128], P('bx', 'by'), may hold values from -0.5 to 0.5
- target_eval: bfloat16 [64, 128, 128, 128], P('bx', 'by'), may hold values from -0.5 to 0.5
- translations: bfloat16 [40, 128, 128], replicated, may hold values from -0.109375 to 0.109375
- shift_up: bfloat16 [2, 2, 128, 128], replicated, may hold values from -0.25 to 0.25
Outputs:
- potential: bfloat16 [64, 128, 32, 128], P('bx', 'by')
- adjoint_out: bfloat16 [64, 128, 32, 128], P('bx', 'by')
The draws below stay inside these ranges and needn't reach their ends.
All inputs are finite; a program needn't handle non-finite values. No bound on the sum of `near_mask` on one device may be relied on, other than what follows from the above.
Results may differ from the reference program's by a relative error of at most 0.01.
Values may be sent and summed in bfloat16 or wider, within the bound.
A program may use at most 256 MiB of HBM per device.

```python
import math
import jax
import jax.numpy as jnp

P_SIZE = 128
NC = 32
Q = 128
NEAR = 9
PAIRS = 40
NBX = 64
NBY = 128


def set_ends(drawn, rng, least, high):
    spot = [jax.random.randint(jax.random.fold_in(rng, axis), (), 0, length) for axis, length in enumerate(drawn.shape)]
    main_axis = drawn.shape.index(max(drawn.shape))
    next_to = spot[:main_axis] + [(spot[main_axis] + 1) % drawn.shape[main_axis]] + spot[main_axis + 1:]
    return drawn.at[tuple(spot)].set(least).at[tuple(next_to)].set(high)


def steps_of(key, dims, cuts, least, largest):
    gain, own = 1.0, jax.random.fold_in(key, 6)
    for axis_at, parts in cuts:
        heights = jnp.exp(jax.random.uniform(jax.random.fold_in(own, axis_at), (parts,), jnp.float32, least / len(cuts), largest / len(cuts)))
        gain = gain * jnp.repeat(heights, dims[axis_at] // parts).reshape([-1 if axis == axis_at else 1 for axis in range(len(dims))])
    return gain


def normal_values(rng, dims, scale, reach, cuts=(), kind=jnp.bfloat16):
    values = jax.random.normal(rng, dims, jnp.float32) * scale
    if len(cuts) > 0:
        values = steps_of(rng, dims, cuts, -0.22, 0.18) * values
    return jnp.clip(values, min=-reach, max=reach).astype(kind)


def setup_inputs(seed: int = 0) -> dict:
    arg_keys = jax.random.split(jax.random.key(seed), 10)
    excitation = normal_values(arg_keys[0], (NBX, NBY, NC, P_SIZE), 1.0, 6.0, ((0, 8), (1, 16)))
    area = jnp.clip(jnp.exp(math.log(8.0) - 2.0794415 * jax.random.uniform(arg_keys[1], (NBX, NBY, P_SIZE), jnp.float32) ** steps_of(arg_keys[1], (NBX, NBY, P_SIZE), ((0, 8), (1, 16)), -0.2, 0.2)), 1.0, 8.0).astype(jnp.bfloat16)
    conductor = set_ends(jax.random.randint(arg_keys[2], (NBX, NBY, P_SIZE), 0, NC), jax.random.fold_in(arg_keys[2], 1), 0, NC - 1).astype(jnp.int32)
    near_blocks = normal_values(arg_keys[3], (NBX, NBY, NEAR, P_SIZE, P_SIZE), (9 * P_SIZE) ** -0.5, 0.1875, ((0, 8), (1, 16)))
    near_mask = set_ends((jax.random.randint(arg_keys[4], (NBX, NBY, NEAR), 0, 4) < 3).astype(jnp.int32), jax.random.fold_in(arg_keys[4], 1), 0, 1)
    source_moments = normal_values(arg_keys[5], (NBX, NBY, Q, P_SIZE), P_SIZE ** -0.5, 0.5, ((0, 8), (1, 16)))
    target_eval = normal_values(arg_keys[6], (NBX, NBY, P_SIZE, Q), Q ** -0.5, 0.5, ((0, 8), (1, 16)))
    translations = normal_values(arg_keys[7], (PAIRS, Q, Q), (27 * Q) ** -0.5, 0.109375)
    shift_up = normal_values(arg_keys[8], (2, 2, Q, Q), (4 * Q) ** -0.5, 0.25)
    return {"excitation": excitation, "area": area, "conductor": conductor, "near_blocks": near_blocks, "near_mask": near_mask, "source_moments": source_moments, "target_eval": target_eval, "translations": translations, "shift_up": shift_up}


def far_pairs():
    listed = []
    for shift_x in range(-3, 4):
        for shift_y in range(-3, 4):
            if max(abs(shift_x), abs(shift_y)) >= 2:
                listed.append((shift_x, shift_y))
    return listed


def near_pairs():
    return [(shift_x, shift_y) for shift_x in (-1, 0, 1) for shift_y in (-1, 0, 1)]


def admitted(parity, offset):
    return -2 <= parity + offset <= 3


def upward(moments, shift_up):
    size_x = moments.shape[0] // 2
    size_y = moments.shape[1] // 2
    blocked = moments.reshape(size_x, 2, size_y, 2, moments.shape[2], moments.shape[3]).astype(jnp.float32)
    summed = jnp.einsum("uavbcq,abpq->uvcp", blocked, shift_up.astype(jnp.float32))
    return summed.astype(jnp.bfloat16)


def downward(expansion, shift_up):
    spread = jnp.einsum("uvcp,abpq->uavbcq", expansion.astype(jnp.float32), shift_up.astype(jnp.float32))
    return spread.reshape(2 * expansion.shape[0], 2 * expansion.shape[1], expansion.shape[2], shift_up.shape[3])


def pair_term(source, translations, shift_x, shift_y, adjoint):
    listed = far_pairs()
    if adjoint:
        operator = translations[listed.index((-shift_x, -shift_y))].astype(jnp.float32)
        return jnp.einsum("uvcq,qp->uvcp", source, operator)
    operator = translations[listed.index((shift_x, shift_y))].astype(jnp.float32)
    return jnp.einsum("uvcq,pq->uvcp", source, operator)


def interact_even(moments, translations, adjoint):
    padded = jnp.pad(moments, ((3, 3), (3, 3), (0, 0), (0, 0))).astype(jnp.float32)
    inner_x = moments.shape[0]
    inner_y = moments.shape[1]
    row_blocks = []
    for row_par in range(2):
        col_blocks = []
        for col_par in range(2):
            summed = jnp.zeros((inner_x // 2, inner_y // 2, moments.shape[2], translations.shape[1]), jnp.float32)
            for shift_x, shift_y in far_pairs():
                if admitted(row_par, shift_x) and admitted(col_par, shift_y):
                    first_x = 3 + row_par + shift_x
                    first_y = 3 + col_par + shift_y
                    source = padded[first_x:first_x + inner_x - 1:2, first_y:first_y + inner_y - 1:2]
                    summed = summed + pair_term(source, translations, shift_x, shift_y, adjoint)
            col_blocks.append(summed)
        row_blocks.append(jnp.stack(col_blocks, axis=2))
    merged = jnp.stack(row_blocks, axis=1)
    return merged.reshape(inner_x, inner_y, moments.shape[2], translations.shape[1])


def far_field(leaf_moments, translations, shift_up, adjoint):
    levels = [leaf_moments]
    levels.append(upward(levels[-1], shift_up))
    levels.append(upward(levels[-1], shift_up))
    while min(levels[-1].shape[0], levels[-1].shape[1]) > 2:
        levels.append(upward(levels[-1], shift_up))
    expansion = None
    for moments in reversed(levels):
        gained = interact_even(moments, translations, adjoint)
        if expansion is not None:
            gained = gained + downward(expansion.astype(jnp.bfloat16), shift_up)
        expansion = gained
    return expansion.astype(jnp.bfloat16)


def reference(excitation, area, conductor, near_blocks, near_mask, source_moments, target_eval, translations, shift_up):
    size_x, size_y, columns, panels = excitation.shape
    labels = jnp.arange(columns, dtype=jnp.int32)
    chosen = (conductor[:, :, None, :] == labels[None, None, :, None]).astype(jnp.float32)
    weights = (area[:, :, None, :].astype(jnp.float32) * chosen).astype(jnp.bfloat16)
    weights_wide = weights.astype(jnp.float32)
    excite_wide = excitation.astype(jnp.float32)
    excite_pad = jnp.pad(excite_wide, ((1, 1), (1, 1), (0, 0), (0, 0)))
    near_fwd = jnp.zeros((size_x, size_y, columns, panels), jnp.float32)
    returned = jnp.zeros((size_x + 2, size_y + 2, columns, panels), jnp.float32)
    for number, (shift_x, shift_y) in enumerate(near_pairs()):
        blocks = near_blocks[:, :, number].astype(jnp.float32)
        kept_mask = near_mask[:, :, number].astype(jnp.float32)[:, :, None, None]
        source = excite_pad[1 + shift_x:1 + shift_x + size_x, 1 + shift_y:1 + shift_y + size_y]
        near_fwd = near_fwd + kept_mask * jnp.einsum("xycs,xyps->xycp", source, blocks)
        product_term = kept_mask * jnp.einsum("xycp,xyps->xycs", weights_wide, blocks)
        returned = returned + jnp.pad(product_term, ((1 + shift_x, 1 - shift_x), (1 + shift_y, 1 - shift_y), (0, 0), (0, 0)))
    near_adj = returned[1:-1, 1:-1]
    moments_fwd = jnp.einsum("xycs,xyqs->xycq", excite_wide, source_moments.astype(jnp.float32)).astype(jnp.bfloat16)
    moments_adj = jnp.einsum("xycp,xypq->xycq", weights_wide, target_eval.astype(jnp.float32)).astype(jnp.bfloat16)
    local_fwd = far_field(moments_fwd, translations, shift_up, False)
    local_adj = far_field(moments_adj, translations, shift_up, True)
    far_fwd = jnp.einsum("xycq,xypq->xycp", local_fwd.astype(jnp.float32), target_eval.astype(jnp.float32))
    far_adj = jnp.einsum("xycq,xyqs->xycs", local_adj.astype(jnp.float32), source_moments.astype(jnp.float32))
    return (near_fwd + far_fwd).astype(jnp.bfloat16), (near_adj + far_adj).astype(jnp.bfloat16)
```

```python
import jax
import jax.numpy as jnp
from jax import lax
from jax.experimental import pallas as pl
from jax.experimental.pallas import tpu as pltpu
from jax.sharding import PartitionSpec as P

MESH = pl.DeviceIdType.MESH
F32 = jnp.float32
BF16 = jnp.bfloat16
DIRS = [(dx, dy) for dx in (-1, 0, 1) for dy in (-1, 0, 1) if (dx, dy) != (0, 0)]
NEAR = [(dx, dy) for dx in (-1, 0, 1) for dy in (-1, 0, 1)]
FAR = [(dx, dy) for dx in range(-3, 4) for dy in range(-3, 4) if max(abs(dx), abs(dy)) >= 2]
OFF1, OFF2, OFF3, OFF4, OFF5, ROWS = 512, 640, 672, 704, 736, 768


def nt(a, b):
    return lax.dot_general(a, b, (((1,), (1,)), ((), ())), preferred_element_type=F32)


def nn(a, b):
    return jnp.dot(a, b, preferred_element_type=F32)


def edge(step, size, width):
    if step == 0:
        return pl.ds(width, size), pl.ds(width, size)
    if step > 0:
        return pl.ds(size, width), pl.ds(0, width)
    return pl.ds(width, width), pl.ds(size + width, width)


def kernel(
    n_rows,
    n_cols,
    exc_hbm,
    area_hbm,
    cond_hbm,
    nb_hbm,
    mask_ref,
    sm_hbm,
    te_hbm,
    tr_hbm,
    su_hbm,
    pot_ref,
    adj_ref,
    epad,
    area_v,
    cond_v,
    nb_v,
    sm_v,
    te_v,
    tr_v,
    su_v,
    wts,
    leaf,
    l1,
    l2,
    l3,
    l4,
    l5,
    nf,
    acc,
    ret_row,
    ret_col,
    ret_cor,
    in_row,
    in_col,
    in_cor,
    wt,
    gain,
    sel5,
    sel4,
    sel3,
    loc2,
    loc1,
    locl,
    in_sem,
    map_sem,
    nb_sem,
    hs_sem,
    hr_sem,
    s3_sem,
    r3_sem,
    s3c_sem,
    r3c_sem,
    s4_sem,
    r4_sem,
):
    r = lax.axis_index("bx")
    c = lax.axis_index("by")
    r2, c2 = r // 2, c // 2
    r4, c4 = r // 4, c // 4

    cp_exc = pltpu.make_async_copy(exc_hbm, epad.at[1:9, 1:9], in_sem.at[0])
    cp_area = pltpu.make_async_copy(area_hbm, area_v, in_sem.at[1])
    cp_cond = pltpu.make_async_copy(cond_hbm, cond_v, in_sem.at[2])
    cp_su = pltpu.make_async_copy(su_hbm, su_v, in_sem.at[3])
    cp_tr = pltpu.make_async_copy(tr_hbm, tr_v, in_sem.at[4])

    def cp_sm(x):
        return pltpu.make_async_copy(sm_hbm.at[x], sm_v.at[x], map_sem.at[0, x])

    def cp_te(x):
        return pltpu.make_async_copy(te_hbm.at[x], te_v.at[x], map_sem.at[1, x])

    def cp_nb(x):
        return pltpu.make_async_copy(nb_hbm.at[x], nb_v.at[x], nb_sem.at[x])

    cp_exc.start()
    cp_area.start()
    cp_cond.start()
    for x in range(8):
        cp_sm(x).start()
        cp_te(x).start()
    cp_su.start()
    for x in range(8):
        cp_nb(x).start()
    cp_tr.start()

    def clear(ref, rows, cols, width, wide):
        ref[0:width] = jnp.zeros((width,) + ref.shape[1:], ref.dtype)
        ref[rows + width :] = jnp.zeros((width,) + ref.shape[1:], ref.dtype)
        side = jnp.zeros((rows, wide) + ref.shape[2:], ref.dtype)
        ref[width : rows + width, 0:wide] = side
        ref[width : rows + width, cols + wide :] = side

    clear(epad, 8, 8, 1, 1)
    clear(leaf, 8, 4, 2, 1)
    clear(l1, 4, 2, 2, 1)
    clear(l2, 2, 1, 2, 1)
    for ref in (l3, l4, l5, in_row, in_col, in_cor, acc):
        ref[...] = jnp.zeros(ref.shape, ref.dtype)

    def inside(row, col):
        return (row >= 0) & (row < n_rows) & (col >= 0) & (col < n_cols)

    def row_peers():
        return [(row, row != r) for row in range(n_rows)]

    def col_peers():
        base = 2 * c2 - 2
        return [
            (j, base + j, (base + j != c) & (base + j >= 0) & (base + j < n_cols)) for j in range(6)
        ]

    def pair_peers():
        return [(v, 2 * v + c % 2, v != c2) for v in range(n_cols // 2)]

    barrier = pltpu.get_barrier_semaphore()
    greeted = jnp.int32(0)

    def greet(row, col, present):
        @pl.when(present)
        def _():
            pl.semaphore_signal(barrier, inc=1, device_id=(row, col), device_id_type=MESH)

        return present.astype(jnp.int32)

    for dx, dy in DIRS:
        greeted = greeted + greet(r + dx, c + dy, inside(r + dx, c + dy))
    for row, present in row_peers():
        greeted = greeted + greet(jnp.int32(row), c, present)
    for _, col, present in col_peers():
        greeted = greeted + greet(r, col, present)
    for _, col, present in pair_peers():
        greeted = greeted + greet(r, col, present)
    pl.semaphore_wait(barrier, greeted)

    def message(number, direction):
        dx, dy = DIRS[direction]
        if number == 4:
            if dy == 0:
                place = 0 if dx > 0 else 1
                return ret_row.at[place], in_row.at[place]
            if dx == 0:
                place = 0 if dy > 0 else 1
                return ret_col.at[place], in_col.at[place]
            place = (0 if dx > 0 else 2) + (0 if dy > 0 else 1)
            return ret_cor.at[place], in_cor.at[place]
        ref, rows, width, cols, wide = (
            (epad, 8, 1, 8, 1),
            (leaf, 8, 2, 4, 1),
            (l1, 4, 2, 2, 1),
            (l2, 2, 2, 1, 1),
        )[number]
        src_rows, dst_rows = edge(dx, rows, width)
        src_cols, dst_cols = edge(dy, cols, wide)
        return ref.at[src_rows, src_cols], ref.at[dst_rows, dst_cols]

    def halo_copy(number, direction):
        dx, dy = DIRS[direction]
        src, dst = message(number, direction)
        return pltpu.make_async_remote_copy(
            src_ref=src,
            dst_ref=dst,
            send_sem=hs_sem.at[number, direction],
            recv_sem=hr_sem.at[number, direction],
            device_id=(r + dx, c + dy),
            device_id_type=MESH,
        )

    def halo_start(number):
        for direction, (dx, dy) in enumerate(DIRS):

            @pl.when(inside(r + dx, c + dy))
            def _():
                halo_copy(number, direction).start()

    def halo_received(number):
        for direction, (dx, dy) in enumerate(DIRS):

            @pl.when(inside(r - dx, c - dy))
            def _():
                halo_copy(number, direction).wait_recv()

    def halo_sent(number):
        for direction, (dx, dy) in enumerate(DIRS):

            @pl.when(inside(r + dx, c + dy))
            def _():
                halo_copy(number, direction).wait_send()

    def l3_row_copy(row, sender):
        return pltpu.make_async_remote_copy(
            src_ref=l3.at[2 + c % 2, sender + 2],
            dst_ref=l3.at[2 + c % 2, sender + 2],
            send_sem=s3_sem.at[row],
            recv_sem=r3_sem.at[sender],
            device_id=(jnp.int32(row), c),
            device_id_type=MESH,
        )

    def l3_col_copy(j, col):
        return pltpu.make_async_remote_copy(
            src_ref=l3.at[2 + c % 2],
            dst_ref=l3.at[c - (2 * (col // 2) - 2)],
            send_sem=s3c_sem.at[j],
            recv_sem=r3c_sem.at[c - (2 * (col // 2) - 2)],
            device_id=(r, col),
            device_id_type=MESH,
        )

    def l3_col_wait(j, col):
        return pltpu.make_async_remote_copy(
            src_ref=l3.at[2 + c % 2],
            dst_ref=l3.at[j],
            send_sem=s3c_sem.at[j],
            recv_sem=r3c_sem.at[j],
            device_id=(r, col),
            device_id_type=MESH,
        )

    def l4_copy(v, col, owner):
        return pltpu.make_async_remote_copy(
            src_ref=l4.at[owner + 2, pl.ds(2, n_rows // 2)],
            dst_ref=l4.at[owner + 2, pl.ds(2, n_rows // 2)],
            send_sem=s4_sem.at[v],
            recv_sem=r4_sem.at[owner],
            device_id=(r, col),
            device_id_type=MESH,
        )

    cp_exc.wait()
    halo_start(0)
    cp_area.wait()
    cp_cond.wait()

    labels = lax.broadcasted_iota(jnp.int32, (32, 128), 0)

    def moments(x, carry):
        cp_sm(x).wait()
        cp_te(x).wait()
        conds = cond_v[x]
        areas = area_v[x].astype(F32)
        for y in range(8):
            half = slice((y % 2) * 128, (y % 2) * 128 + 128)
            chosen = labels == conds[y : y + 1]
            w = jnp.where(chosen, areas[y : y + 1], 0.0).astype(BF16)
            wts[x, y] = w
            leaf[x + 2, 1 + y // 2, 0, :, half] = nt(epad[x + 1, y + 1], sm_v[x, y]).astype(BF16)
            leaf[x + 2, 1 + y // 2, 1, :, half] = nn(w, te_v[x, y]).astype(BF16)
        return carry

    lax.fori_loop(0, 8, moments, 0)

    cp_su.wait()
    ups = [jnp.concatenate([su_v[a, 0], su_v[a, 1]], axis=1) for a in range(2)]

    for u in range(4):
        total = sum(nt(leaf[2 * u + a + 2, 1:5].reshape(256, 256), ups[a]) for a in range(2))
        made = total.astype(BF16).reshape(4, 2, 32, 128)
        for v in range(4):
            l1[u + 2, 1 + v // 2, :, :, (v % 2) * 128 : (v % 2) * 128 + 128] = made[v]
    total = sum(
        nt(jnp.concatenate([l1[2 * u + a + 2, 1:3].reshape(128, 256) for u in range(2)]), ups[a])
        for a in range(2)
    )
    made = total.astype(BF16).reshape(2, 2, 2, 32, 128)
    for u in range(2):
        for v in range(2):
            l2[u + 2, 1, :, :, v * 128 : v * 128 + 128] = made[u, v]
    total = sum(nt(l2[a + 2, 1].reshape(64, 256), ups[a]) for a in range(2))
    l3[2 + c % 2, r + 2] = total.astype(BF16).reshape(2, 32, 128)

    for row, present in row_peers():

        @pl.when(present)
        def _():
            l3_row_copy(row, r).start()

    halo_start(3)
    halo_start(2)
    halo_start(1)

    halo_received(0)

    def near(x, carry):
        cp_nb(x).wait()
        for y in range(8):
            blocks = jnp.concatenate([nb_v[x, y, k] for k in range(9)], axis=1)
            keep = [mask_ref[x, y, k].astype(F32) for k in range(9)]
            source = jnp.concatenate(
                [
                    (epad[x + 1 + dx, y + 1 + dy].astype(F32) * keep[k]).astype(BF16)
                    for k, (dx, dy) in enumerate(NEAR)
                ],
                axis=1,
            )
            nf[x, y] = nt(source, blocks)
            back = nn(wts[x, y], blocks)
            for k, (dx, dy) in enumerate(NEAR):
                acc[x + 1 + dx, y + 1 + dy] += keep[k] * back[:, k * 128 : k * 128 + 128]
        return carry

    lax.fori_loop(0, 2, near, 0)

    for row, present in row_peers():

        @pl.when(present)
        def _():
            l3_row_copy(row, jnp.int32(row)).wait_recv()

    for j, col, present in col_peers():

        @pl.when(present)
        def _():
            l3_col_copy(j, col).start()

    lax.fori_loop(2, 4, near, 0)

    for j, col, present in col_peers():

        @pl.when(present)
        def _():
            l3_col_wait(j, col).wait_recv()

    def up_strip(ref, col, rows):
        total = 0.0
        for a in range(2):
            pairs = [
                jnp.concatenate(
                    [
                        ref[col, 2 * u + a + 2].reshape(64, 128),
                        ref[col + 1, 2 * u + a + 2].reshape(64, 128),
                    ],
                    axis=1,
                )
                for u in range(rows)
            ]
            total = total + nt(jnp.concatenate(pairs, axis=0), ups[a])
        return total.astype(BF16).reshape(rows, 2, 32, 128)

    l4[c2 + 2, 2 : 2 + n_rows // 2] = up_strip(l3, 2, n_rows // 2)
    for v, col, present in pair_peers():

        @pl.when(present)
        def _():
            l4_copy(v, col, c2).start()

    lax.fori_loop(4, 6, near, 0)

    for v, col, present in pair_peers():

        @pl.when(present)
        def _():
            l4_copy(v, col, jnp.int32(v)).wait_recv()

    for col in range(n_cols // 4):
        l5[col + 2, 2 : 2 + n_rows // 4] = up_strip(l4, 2 + 2 * col, n_rows // 4)

    lax.fori_loop(6, 8, near, 0)

    for place, row in ((0, 9), (1, 0)):
        ret_row[place] = acc[row, 1:9].astype(BF16)
        ret_col[place] = acc[1:9, row].astype(BF16)
        for other, col in ((0, 9), (1, 0)):
            ret_cor[2 * place + other] = acc[row, col].astype(BF16)
    halo_start(4)

    cp_tr.wait()
    for dx in range(-3, 4):
        for dy in range(-1, 2):
            for i in range(2):
                for j in range(2):
                    offset = (dx, 2 * dy + j - i)
                    block = (
                        tr_v[FAR.index(offset)] if offset in FAR else jnp.zeros((128, 128), BF16)
                    )
                    wt[
                        3 * (dx + 3) + dy + 1,
                        i * 128 : i * 128 + 128,
                        j * 128 : j * 128 + 128,
                    ] = block

    halo_received(3)
    halo_received(2)
    halo_received(1)

    def sources(side, a, dx, dy):
        parts = []
        for i in range(4):
            parts.append(leaf[2 * i + a + dx + 2, 1 + dy : 5 + dy, side].reshape(128, 256))
        for i in range(2):
            parts.append(l1[2 * i + a + dx + 2, 1 + dy : 3 + dy, side].reshape(64, 256))
        parts.append(l2[a + dx + 2, 1 + dy, side])
        for ref, row, col in (
            (l3, 2 * r2, 0),
            (l4, 2 * r4, 2 * c4),
            (l5, 0, 2 * (c // 8)),
        ):
            row = row + a + dx + 2
            col = col + 2 * (1 + dy)
            parts.append(jnp.concatenate([ref[col, row, side], ref[col + 1, row, side]], axis=1))
        return jnp.concatenate(parts, axis=0)

    def interact(side, a, dx, columns):
        taken = jnp.concatenate([sources(side, a, dx, dy) for dy in columns], axis=1)
        if side == 0:
            tiles = [wt[3 * (dx + 3) + dy + 1] for dy in columns]
            return nt(taken, jnp.concatenate(tiles, axis=1))
        tiles = [wt[3 * (3 - dx) + 1 - dy] for dy in columns]
        return nn(taken, jnp.concatenate(tiles, axis=0))

    for side in range(2):
        for a in range(2):
            gain[side, a] = jnp.zeros((ROWS, 256), F32)

            def outer(i, carry):
                dx = i - 3 + 3 * (i // 2) if a == 1 else i + 1 - 3 * ((2 - i) // 2)
                gain[side, a] += interact(side, a, dx, (-1, 0, 1))
                return carry

            def inner(i, carry):
                gain[side, a] += interact(side, a, i - 1, (-1, 1))
                return carry

            lax.fori_loop(0, 3, outer, 0)
            lax.fori_loop(0, 3, inner, 0)

    for a in range(2):
        for side in range(2):
            top = gain[side, a, OFF5 : OFF5 + 32].astype(BF16)
            for b in range(2):
                sel5[a, b, side] = top[:, b * 128 : b * 128 + 128]
    parent = sel5[r4, c4 % 2].reshape(64, 128)
    for off, sel, row, col in (
        (OFF4, sel4, r2 % 2, c2 % 2),
        (OFF3, sel3, r % 2, c % 2),
        (OFF2, loc2, None, None),
    ):
        for a in range(2):
            spread = nn(parent, ups[a])
            for side in range(2):
                made = spread[side * 32 : side * 32 + 32] + gain[side, a, off : off + 32]
                made = made.astype(BF16)
                for b in range(2):
                    sel[a, b, side] = made[:, b * 128 : b * 128 + 128]
        if row is not None:
            parent = sel[row, col].reshape(64, 128)

    for upper, lower, count, off in ((loc2, loc1, 2, OFF1), (loc1, locl, 4, 0)):
        for u in range(count):
            for a in range(2):
                spread = nn(upper[u].reshape(count * 64, 128), ups[a])
                for v in range(count):
                    for side in range(2):
                        first = v * 64 + side * 32
                        at = off + (u * count + v) * 32
                        made = spread[first : first + 32] + gain[side, a, at : at + 32]
                        made = made.astype(BF16)
                        for b in range(2):
                            lower[2 * u + a, 2 * v + b, side] = made[:, b * 128 : b * 128 + 128]

    halo_received(4)
    for place, row in ((0, 1), (1, 8)):
        acc[row, 1:9] += in_row[place].astype(F32)
        acc[1:9, row] += in_col[place].astype(F32)
        for other, col in ((0, 1), (1, 8)):
            acc[row, col] += in_cor[2 * place + other].astype(F32)

    def finish(x, carry):
        for y in range(8):
            pot_ref[x, y] = (nf[x, y] + nt(locl[x, y, 0], te_v[x, y])).astype(BF16)
            adj_ref[x, y] = (acc[x + 1, y + 1] + nn(locl[x, y, 1], sm_v[x, y])).astype(BF16)
        return carry

    lax.fori_loop(0, 8, finish, 0)

    for number in range(5):
        halo_sent(number)
    for row, present in row_peers():

        @pl.when(present)
        def _():
            l3_row_copy(row, r).wait_send()

    for j, col, present in col_peers():

        @pl.when(present)
        def _():
            l3_col_copy(j, col).wait_send()

    for v, col, present in pair_peers():

        @pl.when(present)
        def _():
            l4_copy(v, col, c2).wait_send()


def solution(mesh):
    n_rows, n_cols = mesh.shape["bx"], mesh.shape["by"]
    hbm = pl.BlockSpec(memory_space=pl.ANY)
    vmem = pl.BlockSpec(memory_space=pltpu.VMEM)
    smem = pl.BlockSpec(memory_space=pltpu.SMEM)
    box = (2, 32, 128)
    pair = (2, 32, 256)
    scratch = [
        pltpu.VMEM((10, 10, 32, 128), BF16),
        pltpu.VMEM((8, 8, 128), BF16),
        pltpu.VMEM((8, 8, 128), jnp.int32),
        pltpu.VMEM((8, 8, 9, 128, 128), BF16),
        pltpu.VMEM((8, 8, 128, 128), BF16),
        pltpu.VMEM((8, 8, 128, 128), BF16),
        pltpu.VMEM((40, 128, 128), BF16),
        pltpu.VMEM((2, 2, 128, 128), BF16),
        pltpu.VMEM((8, 8, 32, 128), BF16),
        pltpu.VMEM((12, 6) + pair, BF16),
        pltpu.VMEM((8, 4) + pair, BF16),
        pltpu.VMEM((6, 3) + pair, BF16),
        pltpu.VMEM((6, n_rows + 4) + box, BF16),
        pltpu.VMEM((n_cols // 2 + 4, n_rows // 2 + 4) + box, BF16),
        pltpu.VMEM((n_cols // 4 + 4, n_rows // 4 + 4) + box, BF16),
        pltpu.VMEM((8, 8, 32, 128), F32),
        pltpu.VMEM((10, 10, 32, 128), F32),
        pltpu.VMEM((2, 8, 32, 128), BF16),
        pltpu.VMEM((2, 8, 32, 128), BF16),
        pltpu.VMEM((4, 32, 128), BF16),
        pltpu.VMEM((2, 8, 32, 128), BF16),
        pltpu.VMEM((2, 8, 32, 128), BF16),
        pltpu.VMEM((4, 32, 128), BF16),
        pltpu.VMEM((21, 256, 256), BF16),
        pltpu.VMEM((2, 2, ROWS, 256), F32),
        pltpu.VMEM((2, 2) + box, BF16),
        pltpu.VMEM((2, 2) + box, BF16),
        pltpu.VMEM((2, 2) + box, BF16),
        pltpu.VMEM((2, 2) + box, BF16),
        pltpu.VMEM((4, 4) + box, BF16),
        pltpu.VMEM((8, 8) + box, BF16),
        pltpu.SemaphoreType.DMA((5,)),
        pltpu.SemaphoreType.DMA((2, 8)),
        pltpu.SemaphoreType.DMA((8,)),
        pltpu.SemaphoreType.DMA((5, 8)),
        pltpu.SemaphoreType.DMA((5, 8)),
        pltpu.SemaphoreType.DMA((n_rows,)),
        pltpu.SemaphoreType.DMA((n_rows,)),
        pltpu.SemaphoreType.DMA((6,)),
        pltpu.SemaphoreType.DMA((6,)),
        pltpu.SemaphoreType.DMA((n_cols // 2,)),
        pltpu.SemaphoreType.DMA((n_cols // 2,)),
    ]

    def per_device(*arrays):
        def body(*refs):
            kernel(n_rows, n_cols, *refs)

        result = jax.ShapeDtypeStruct(arrays[0].shape, BF16)
        return pl.pallas_call(
            body,
            out_shape=(result, result),
            in_specs=[hbm, hbm, hbm, hbm, smem, hbm, hbm, hbm, hbm],
            out_specs=(vmem, vmem),
            scratch_shapes=scratch,
            compiler_params=pltpu.CompilerParams(
                collective_id=0, has_side_effects=True, vmem_limit_bytes=56 * 1024 * 1024
            ),
            cost_estimate=pl.CostEstimate(
                flops=4300000000, bytes_accessed=26000000, transcendentals=0
            ),
            name="fmm",
        )(*arrays)

    placed = (
        P("bx", "by", None, None),
        P("bx", "by", None),
        P("bx", "by", None),
        P("bx", "by", None, None, None),
        P("bx", "by", None),
        P("bx", "by", None, None),
        P("bx", "by", None, None),
        P(),
        P(),
    )
    return jax.shard_map(
        per_device,
        mesh=mesh,
        in_specs=placed,
        out_specs=(P("bx", "by", None, None), P("bx", "by", None, None)),
        check_vma=False,
    )
```

```python
import jax
import jax.numpy as jnp
from jax import lax
from jax.experimental import pallas as pl
from jax.experimental.pallas import tpu as pltpu
from jax.sharding import PartitionSpec as P

MESH = pl.DeviceIdType.MESH
F32 = jnp.float32
BF16 = jnp.bfloat16
DIRS = [(dx, dy) for dx in (-1, 0, 1) for dy in (-1, 0, 1) if (dx, dy) != (0, 0)]
NEAR = [(dx, dy) for dx in (-1, 0, 1) for dy in (-1, 0, 1)]
FAR = [(dx, dy) for dx in range(-3, 4) for dy in range(-3, 4) if max(abs(dx), abs(dy)) >= 2]
OFF1, OFF2, OFF3, OFF4, OFF5, ROWS = 512, 640, 672, 704, 736, 768


def nt(a, b):
    return lax.dot_general(a, b, (((1,), (1,)), ((), ())), preferred_element_type=F32)


def nn(a, b):
    return jnp.dot(a, b, preferred_element_type=F32)


def edge(step, size, width):
    if step == 0:
        return pl.ds(width, size), pl.ds(width, size)
    if step > 0:
        return pl.ds(size, width), pl.ds(0, width)
    return pl.ds(width, width), pl.ds(size + width, width)


def kernel(
    n_rows,
    n_cols,
    exc_hbm,
    area_hbm,
    cond_hbm,
    nb_hbm,
    mask_ref,
    sm_hbm,
    te_hbm,
    tr_hbm,
    su_hbm,
    pot_ref,
    adj_ref,
    epad,
    area_v,
    cond_v,
    nb_v,
    sm_v,
    te_v,
    tr_v,
    su_v,
    wts,
    leaf,
    l1,
    l2,
    l3,
    l4,
    l5,
    nf,
    acc,
    ret_row,
    ret_col,
    in_row,
    in_col,
    wt,
    gain,
    sel5,
    sel4,
    sel3,
    loc2,
    loc1,
    locl,
    in_sem,
    map_sem,
    nb_sem,
    hs_sem,
    hr_sem,
    s3_sem,
    r3_sem,
    sp_sem,
    rp_sem,
    s4_sem,
    r4_sem,
):
    r = lax.axis_index("bx")
    c = lax.axis_index("by")
    r2, c2 = r // 2, c // 2
    r4, c4 = r // 4, c // 4

    cp_exc = pltpu.make_async_copy(exc_hbm, epad.at[1:9, 1:9], in_sem.at[0])
    cp_area = pltpu.make_async_copy(area_hbm, area_v, in_sem.at[1])
    cp_cond = pltpu.make_async_copy(cond_hbm, cond_v, in_sem.at[2])
    cp_su = pltpu.make_async_copy(su_hbm, su_v, in_sem.at[3])
    cp_tr = pltpu.make_async_copy(tr_hbm, tr_v, in_sem.at[4])

    def cp_sm(x):
        return pltpu.make_async_copy(sm_hbm.at[x], sm_v.at[x], map_sem.at[0, x])

    def cp_te(x):
        return pltpu.make_async_copy(te_hbm.at[x], te_v.at[x], map_sem.at[1, x])

    def cp_nb(x):
        return pltpu.make_async_copy(nb_hbm.at[x], nb_v.at[x], nb_sem.at[x])

    cp_exc.start()
    cp_area.start()
    cp_cond.start()
    for x in range(8):
        cp_sm(x).start()
        cp_te(x).start()
    cp_su.start()
    for x in range(8):
        cp_nb(x).start()
    cp_tr.start()

    def clear(ref, rows, cols, width, wide):
        ref[0:width] = jnp.zeros((width,) + ref.shape[1:], ref.dtype)
        ref[rows + width :] = jnp.zeros((width,) + ref.shape[1:], ref.dtype)
        side = jnp.zeros((rows, wide) + ref.shape[2:], ref.dtype)
        ref[width : rows + width, 0:wide] = side
        ref[width : rows + width, cols + wide :] = side

    clear(epad, 8, 8, 1, 1)
    clear(leaf, 8, 4, 2, 1)
    clear(l1, 4, 2, 2, 1)
    clear(l2, 2, 1, 2, 1)
    for ref in (l3, l4, l5, in_row, in_col):
        ref[...] = jnp.zeros(ref.shape, ref.dtype)

    def inside(row, col):
        return (row >= 0) & (row < n_rows) & (col >= 0) & (col < n_cols)

    def row_peers():
        return [(row, row != r) for row in range(n_rows)]

    def pair_peers():
        return [(v, 2 * v + c % 2, v != c2) for v in range(n_cols // 2)]

    barrier = pltpu.get_barrier_semaphore()
    greeted = jnp.int32(0)

    def greet(row, col, present):
        @pl.when(present)
        def _():
            pl.semaphore_signal(barrier, inc=1, device_id=(row, col), device_id_type=MESH)

        return present.astype(jnp.int32)

    for dy in (-1, 1):
        greeted = greeted + greet(r, c + dy, inside(r, c + dy))
    for row, present in row_peers():
        greeted = greeted + greet(jnp.int32(row), c, present)
    for _, col, present in pair_peers():
        greeted = greeted + greet(r, col, present)
    pl.semaphore_wait(barrier, greeted)

    def halo_copy(number, direction):
        dx, dy = DIRS[direction]
        if number == 4:
            place = 0 if dx + dy > 0 else 1
            src, dst = (ret_row, in_row) if dy == 0 else (ret_col, in_col)
            src, dst = src.at[place], dst.at[place]
        else:
            ref, rows, width, cols, wide = (
                (epad, 8, 1, 8, 1),
                (leaf, 8, 2, 4, 1),
                (l1, 4, 2, 2, 1),
                (l2, 2, 2, 1, 1),
            )[number]
            src_rows, dst_rows = edge(dx, rows, width)
            src_cols, dst_cols = edge(dy, cols, wide)
            src = ref.at[src_rows if dy == 0 or dx == 0 else dst_rows, src_cols]
            dst = ref.at[dst_rows, dst_cols]
        return pltpu.make_async_remote_copy(
            src_ref=src,
            dst_ref=dst,
            send_sem=hs_sem.at[number, direction],
            recv_sem=hr_sem.at[number, direction],
            device_id=(r + dx, c) if dy == 0 else (r, c + dy),
            device_id_type=MESH,
        )

    ROW = [i for i, (dx, dy) in enumerate(DIRS) if dy == 0]
    COL = [i for i, (dx, dy) in enumerate(DIRS) if dx == 0]
    CORNER = [i for i, (dx, dy) in enumerate(DIRS) if dx * dy != 0]

    def leaves(direction):
        dx, dy = DIRS[direction]
        if dy == 0:
            return inside(r + dx, c)
        return inside(r - dx, c) & inside(r, c + dy)

    def halo_start(number, directions):
        for direction in directions:

            @pl.when(leaves(direction))
            def _():
                halo_copy(number, direction).start()

    def halo_received(number, directions):
        for direction in directions:
            dx, dy = DIRS[direction]

            @pl.when(inside(r - dx, c - dy))
            def _():
                halo_copy(number, direction).wait_recv()

    def halo_sent(number, directions):
        for direction in directions:

            @pl.when(leaves(direction))
            def _():
                halo_copy(number, direction).wait_send()

    def l3_row_copy(row, sender):
        return pltpu.make_async_remote_copy(
            src_ref=l3.at[2 + c % 2, sender + 2],
            dst_ref=l3.at[2 + c % 2, sender + 2],
            send_sem=s3_sem.at[row],
            recv_sem=r3_sem.at[sender],
            device_id=(jnp.int32(row), c),
            device_id_type=MESH,
        )

    other = c + 1 - 2 * (c % 2)

    def l3_col_copy(step, received=False):
        rows = pl.ds(2, n_rows) if step == 0 else pl.ds(2 * r2, 6)
        own = 2 + c % 2
        there = 2 + (1 - c % 2) if received else own
        if step == 0:
            src, dst, col = own, there, other
        elif step == 1:
            src, dst, col = own, c % 2, c + 2
        elif step == 2:
            src, dst, col = own, 4 + c % 2, c - 2
        else:
            src = c % 2 + (0 if step == 3 else 4)
            dst = (1 - c % 2 if received else c % 2) + (0 if step == 3 else 4)
            col = other
        return pltpu.make_async_remote_copy(
            src_ref=l3.at[src, rows],
            dst_ref=l3.at[dst, rows],
            send_sem=sp_sem.at[step],
            recv_sem=rp_sem.at[step],
            device_id=(r, col),
            device_id_type=MESH,
        )

    has_last, has_next = c2 > 0, c2 < n_cols // 2 - 1
    COL_SENDS = (True, has_next, has_last, has_last, has_next)
    COL_COMES = (True, has_last, has_next, has_last, has_next)

    part = n_rows // 4

    def l4_copy(v, col, owner):
        rows = pl.ds(2 + part * (c % 2), part)
        return pltpu.make_async_remote_copy(
            src_ref=l4.at[owner + 2, rows],
            dst_ref=l4.at[owner + 2, rows],
            send_sem=s4_sem.at[v],
            recv_sem=r4_sem.at[owner],
            device_id=(r, col),
            device_id_type=MESH,
        )

    def l4_pass(half):
        place = l4.at[pl.ds(2, n_cols // 2), pl.ds(2 + part * half, part)]
        return pltpu.make_async_remote_copy(
            src_ref=place,
            dst_ref=place,
            send_sem=sp_sem.at[5],
            recv_sem=rp_sem.at[5],
            device_id=(r, other),
            device_id_type=MESH,
        )

    def l3_col_start(step):
        @pl.when(COL_SENDS[step])
        def _():
            l3_col_copy(step).start()

    def l3_col_received(step):
        @pl.when(COL_COMES[step])
        def _():
            l3_col_copy(step, True).wait_recv()

    cp_exc.wait()
    halo_start(0, ROW + COL)
    acc[...] = jnp.zeros(acc.shape, F32)
    cp_area.wait()
    cp_cond.wait()

    labels = lax.broadcasted_iota(jnp.int32, (32, 128), 0)

    def moments(x, carry):
        cp_sm(x).wait()
        cp_te(x).wait()
        conds = cond_v[x]
        areas = area_v[x].astype(F32)
        for y in range(8):
            half = slice((y % 2) * 128, (y % 2) * 128 + 128)
            chosen = labels == conds[y : y + 1]
            w = jnp.where(chosen, areas[y : y + 1], 0.0).astype(BF16)
            wts[x, y] = w
            leaf[x + 2, 1 + y // 2, 0, :, half] = nt(epad[x + 1, y + 1], sm_v[x, y]).astype(BF16)
            leaf[x + 2, 1 + y // 2, 1, :, half] = nn(w, te_v[x, y]).astype(BF16)
        return carry

    lax.fori_loop(0, 8, moments, 0)

    cp_su.wait()
    ups = [jnp.concatenate([su_v[a, 0], su_v[a, 1]], axis=1) for a in range(2)]

    for u in range(4):
        total = sum(nt(leaf[2 * u + a + 2, 1:5].reshape(256, 256), ups[a]) for a in range(2))
        made = total.astype(BF16).reshape(4, 2, 32, 128)
        for v in range(4):
            l1[u + 2, 1 + v // 2, :, :, (v % 2) * 128 : (v % 2) * 128 + 128] = made[v]
    total = sum(
        nt(jnp.concatenate([l1[2 * u + a + 2, 1:3].reshape(128, 256) for u in range(2)]), ups[a])
        for a in range(2)
    )
    made = total.astype(BF16).reshape(2, 2, 2, 32, 128)
    for u in range(2):
        for v in range(2):
            l2[u + 2, 1, :, :, v * 128 : v * 128 + 128] = made[u, v]
    total = sum(nt(l2[a + 2, 1].reshape(64, 256), ups[a]) for a in range(2))
    l3[2 + c % 2, r + 2] = total.astype(BF16).reshape(2, 32, 128)

    for row, present in row_peers():

        @pl.when(present)
        def _():
            l3_row_copy(row, r).start()

    halo_received(0, ROW)
    halo_start(0, CORNER)
    for number in (3, 2, 1):
        halo_start(number, ROW + COL)

    cp_tr.wait()
    for dx in range(-3, 4):
        for dy in range(-1, 2):
            for i in range(2):
                for j in range(2):
                    offset = (dx, 2 * dy + j - i)
                    block = (
                        tr_v[FAR.index(offset)] if offset in FAR else jnp.zeros((128, 128), BF16)
                    )
                    wt[
                        3 * (dx + 3) + dy + 1,
                        i * 128 : i * 128 + 128,
                        j * 128 : j * 128 + 128,
                    ] = block

    halo_received(0, COL + CORNER)

    def near(x, carry):
        cp_nb(x).wait()
        for y in range(8):
            blocks = jnp.concatenate([nb_v[x, y, k] for k in range(9)], axis=1)
            keep = [mask_ref[x, y, k].astype(F32) for k in range(9)]
            source = jnp.concatenate(
                [
                    (epad[x + 1 + dx, y + 1 + dy].astype(F32) * keep[k]).astype(BF16)
                    for k, (dx, dy) in enumerate(NEAR)
                ],
                axis=1,
            )
            nf[x, y] = nt(source, blocks)
            back = nn(wts[x, y], blocks)
            for k, (dx, dy) in enumerate(NEAR):
                acc[x + 1 + dx, y + 1 + dy] += keep[k] * back[:, k * 128 : k * 128 + 128]
        return carry

    lax.fori_loop(0, 2, near, 0)

    for row, present in row_peers():

        @pl.when(present)
        def _():
            l3_row_copy(row, jnp.int32(row)).wait_recv()

    for step in range(3):
        l3_col_start(step)
    halo_received(3, ROW)
    halo_start(3, CORNER)

    lax.fori_loop(2, 4, near, 0)

    l3_col_received(0)

    def up_strip(ref, col, first, rows):
        total = 0.0
        for a in range(2):
            pairs = [
                jnp.concatenate(
                    [
                        ref[col, first + 2 * u + a].reshape(64, 128),
                        ref[col + 1, first + 2 * u + a].reshape(64, 128),
                    ],
                    axis=1,
                )
                for u in range(rows)
            ]
            total = total + nt(jnp.concatenate(pairs, axis=0), ups[a])
        return total.astype(BF16).reshape(rows, 2, 32, 128)

    l4[c2 + 2, pl.ds(2 + part * (c % 2), part)] = up_strip(l3, 2, 2 + 2 * part * (c % 2), part)
    for v, col, present in pair_peers():

        @pl.when(present)
        def _():
            l4_copy(v, col, c2).start()

    l3_col_received(1)
    l3_col_start(3)
    l3_col_received(2)
    l3_col_start(4)
    halo_received(2, ROW)
    halo_start(2, CORNER)

    lax.fori_loop(4, 6, near, 0)

    halo_received(1, ROW)
    halo_start(1, CORNER)
    for v, col, present in pair_peers():

        @pl.when(present)
        def _():
            l4_copy(v, col, jnp.int32(v)).wait_recv()

    l4_pass(c % 2).start()

    lax.fori_loop(6, 8, near, 0)

    for place, row in ((0, 9), (1, 0)):
        ret_row[place] = acc[row].astype(BF16)
    halo_start(4, ROW)

    l3_col_received(3)
    l3_col_received(4)
    l4_pass(1 - c % 2).wait_recv()
    for col in range(n_cols // 4):
        l5[col + 2, 2 : 2 + n_rows // 4] = up_strip(l4, 2 + 2 * col, 2, n_rows // 4)

    for number in (3, 2, 1):
        halo_received(number, COL + CORNER)

    def sources(side, a, dx, dy):
        parts = []
        for i in range(4):
            parts.append(leaf[2 * i + a + dx + 2, 1 + dy : 5 + dy, side].reshape(128, 256))
        for i in range(2):
            parts.append(l1[2 * i + a + dx + 2, 1 + dy : 3 + dy, side].reshape(64, 256))
        parts.append(l2[a + dx + 2, 1 + dy, side])
        for ref, row, col in (
            (l3, 2 * r2, 0),
            (l4, 2 * r4, 2 * c4),
            (l5, 0, 2 * (c // 8)),
        ):
            row = row + a + dx + 2
            col = col + 2 * (1 + dy)
            parts.append(jnp.concatenate([ref[col, row, side], ref[col + 1, row, side]], axis=1))
        return jnp.concatenate(parts, axis=0)

    def interact(side, a, dx, columns):
        taken = jnp.concatenate([sources(side, a, dx, dy) for dy in columns], axis=1)
        if side == 0:
            tiles = [wt[3 * (dx + 3) + dy + 1] for dy in columns]
            return nt(taken, jnp.concatenate(tiles, axis=1))
        tiles = [wt[3 * (3 - dx) + 1 - dy] for dy in columns]
        return nn(taken, jnp.concatenate(tiles, axis=0))

    for side in range(2):
        for a in range(2):
            gain[side, a] = jnp.zeros((ROWS, 256), F32)

            def outer(i, carry):
                dx = i - 3 + 3 * (i // 2) if a == 1 else i + 1 - 3 * ((2 - i) // 2)
                gain[side, a] += interact(side, a, dx, (-1, 0, 1))
                return carry

            def inner(i, carry):
                gain[side, a] += interact(side, a, i - 1, (-1, 1))
                return carry

            lax.fori_loop(0, 3, outer, 0)
            lax.fori_loop(0, 3, inner, 0)

        if side == 0:
            halo_received(4, ROW)
            for place, row in ((0, 1), (1, 8)):
                acc[row] += in_row[place].astype(F32)
            for place, col in ((0, 9), (1, 0)):
                ret_col[place] = acc[1:9, col].astype(BF16)
            halo_start(4, COL)

    for a in range(2):
        for side in range(2):
            top = gain[side, a, OFF5 : OFF5 + 32].astype(BF16)
            for b in range(2):
                sel5[a, b, side] = top[:, b * 128 : b * 128 + 128]
    parent = sel5[r4, c4 % 2].reshape(64, 128)
    for off, sel, row, col in (
        (OFF4, sel4, r2 % 2, c2 % 2),
        (OFF3, sel3, r % 2, c % 2),
        (OFF2, loc2, None, None),
    ):
        for a in range(2):
            spread = nn(parent, ups[a])
            for side in range(2):
                made = spread[side * 32 : side * 32 + 32] + gain[side, a, off : off + 32]
                made = made.astype(BF16)
                for b in range(2):
                    sel[a, b, side] = made[:, b * 128 : b * 128 + 128]
        if row is not None:
            parent = sel[row, col].reshape(64, 128)

    for upper, lower, count, off in ((loc2, loc1, 2, OFF1), (loc1, locl, 4, 0)):
        for u in range(count):
            for a in range(2):
                spread = nn(upper[u].reshape(count * 64, 128), ups[a])
                for v in range(count):
                    for side in range(2):
                        first = v * 64 + side * 32
                        at = off + (u * count + v) * 32
                        made = spread[first : first + 32] + gain[side, a, at : at + 32]
                        made = made.astype(BF16)
                        for b in range(2):
                            lower[2 * u + a, 2 * v + b, side] = made[:, b * 128 : b * 128 + 128]

    halo_received(4, COL)
    for place, col in ((0, 1), (1, 8)):
        acc[1:9, col] += in_col[place].astype(F32)

    def finish(x, carry):
        for y in range(8):
            pot_ref[x, y] = (nf[x, y] + nt(locl[x, y, 0], te_v[x, y])).astype(BF16)
            adj_ref[x, y] = (acc[x + 1, y + 1] + nn(locl[x, y, 1], sm_v[x, y])).astype(BF16)
        return carry

    lax.fori_loop(0, 8, finish, 0)

    for number in range(5):
        halo_sent(number, ROW + COL + (CORNER if number < 4 else []))
    for row, present in row_peers():

        @pl.when(present)
        def _():
            l3_row_copy(row, r).wait_send()

    for step in range(5):

        @pl.when(COL_SENDS[step])
        def _():
            l3_col_copy(step).wait_send()

    l4_pass(c % 2).wait_send()
    for v, col, present in pair_peers():

        @pl.when(present)
        def _():
            l4_copy(v, col, c2).wait_send()


def solution(mesh):
    n_rows, n_cols = mesh.shape["bx"], mesh.shape["by"]
    hbm = pl.BlockSpec(memory_space=pl.ANY)
    vmem = pl.BlockSpec(memory_space=pltpu.VMEM)
    smem = pl.BlockSpec(memory_space=pltpu.SMEM)
    box = (2, 32, 128)
    pair = (2, 32, 256)
    scratch = [
        pltpu.VMEM((10, 10, 32, 128), BF16),
        pltpu.VMEM((8, 8, 128), BF16),
        pltpu.VMEM((8, 8, 128), jnp.int32),
        pltpu.VMEM((8, 8, 9, 128, 128), BF16),
        pltpu.VMEM((8, 8, 128, 128), BF16),
        pltpu.VMEM((8, 8, 128, 128), BF16),
        pltpu.VMEM((40, 128, 128), BF16),
        pltpu.VMEM((2, 2, 128, 128), BF16),
        pltpu.VMEM((8, 8, 32, 128), BF16),
        pltpu.VMEM((12, 6) + pair, BF16),
        pltpu.VMEM((8, 4) + pair, BF16),
        pltpu.VMEM((6, 3) + pair, BF16),
        pltpu.VMEM((6, n_rows + 4) + box, BF16),
        pltpu.VMEM((n_cols // 2 + 4, n_rows // 2 + 4) + box, BF16),
        pltpu.VMEM((n_cols // 4 + 4, n_rows // 4 + 4) + box, BF16),
        pltpu.VMEM((8, 8, 32, 128), F32),
        pltpu.VMEM((10, 10, 32, 128), F32),
        pltpu.VMEM((2, 10, 32, 128), BF16),
        pltpu.VMEM((2, 8, 32, 128), BF16),
        pltpu.VMEM((2, 10, 32, 128), BF16),
        pltpu.VMEM((2, 8, 32, 128), BF16),
        pltpu.VMEM((21, 256, 256), BF16),
        pltpu.VMEM((2, 2, ROWS, 256), F32),
        pltpu.VMEM((2, 2) + box, BF16),
        pltpu.VMEM((2, 2) + box, BF16),
        pltpu.VMEM((2, 2) + box, BF16),
        pltpu.VMEM((2, 2) + box, BF16),
        pltpu.VMEM((4, 4) + box, BF16),
        pltpu.VMEM((8, 8) + box, BF16),
        pltpu.SemaphoreType.DMA((5,)),
        pltpu.SemaphoreType.DMA((2, 8)),
        pltpu.SemaphoreType.DMA((8,)),
        pltpu.SemaphoreType.DMA((5, 8)),
        pltpu.SemaphoreType.DMA((5, 8)),
        pltpu.SemaphoreType.DMA((n_rows,)),
        pltpu.SemaphoreType.DMA((n_rows,)),
        pltpu.SemaphoreType.DMA((6,)),
        pltpu.SemaphoreType.DMA((6,)),
        pltpu.SemaphoreType.DMA((n_cols // 2,)),
        pltpu.SemaphoreType.DMA((n_cols // 2,)),
    ]

    def per_device(*arrays):
        def body(*refs):
            kernel(n_rows, n_cols, *refs)

        result = jax.ShapeDtypeStruct(arrays[0].shape, BF16)
        made = pl.pallas_call(
            body,
            out_shape=(result, result),
            in_specs=[hbm, hbm, hbm, hbm, smem, hbm, hbm, hbm, hbm],
            out_specs=(vmem, vmem),
            scratch_shapes=scratch,
            compiler_params=pltpu.CompilerParams(
                collective_id=0, has_side_effects=True, vmem_limit_bytes=56 * 1024 * 1024
            ),
            cost_estimate=pl.CostEstimate(
                flops=4300000000, bytes_accessed=26000000, transcendentals=0
            ),
            name="fmm",
        )(*arrays)

        def hand_on(pot_in, adj_in, pot_out, adj_out, held, in_sems, out_sems):
            pairs = []
            for which, (src, dst) in enumerate(((pot_in, pot_out), (adj_in, adj_out))):
                for part in range(4):
                    rows = pl.ds(2 * part, 2)
                    slot = held.at[which, rows]
                    pairs.append(
                        (
                            pltpu.make_async_copy(src.at[rows], slot, in_sems.at[which, part]),
                            pltpu.make_async_copy(slot, dst.at[rows], out_sems.at[which, part]),
                        )
                    )
            for fetch, _ in pairs:
                fetch.start()
            for fetch, store in pairs:
                fetch.wait()
                store.start()
            for _, store in pairs:
                store.wait()

        return pl.pallas_call(
            hand_on,
            out_shape=(result, result),
            in_specs=[hbm, hbm],
            out_specs=(hbm, hbm),
            scratch_shapes=[
                pltpu.VMEM((2,) + arrays[0].shape, BF16),
                pltpu.SemaphoreType.DMA((2, 4)),
                pltpu.SemaphoreType.DMA((2, 4)),
            ],
            cost_estimate=pl.CostEstimate(flops=0, bytes_accessed=2097152, transcendentals=0),
            name="hand_on",
        )(*made)

    placed = (
        P("bx", "by", None, None),
        P("bx", "by", None),
        P("bx", "by", None),
        P("bx", "by", None, None, None),
        P("bx", "by", None),
        P("bx", "by", None, None),
        P("bx", "by", None, None),
        P(),
        P(),
    )
    return jax.shard_map(
        per_device,
        mesh=mesh,
        in_specs=placed,
        out_specs=(P("bx", "by", None, None), P("bx", "by", None, None)),
        check_vma=False,
    )
```

```python
import jax
import jax.numpy as jnp
from jax import lax
from jax.experimental import pallas as pl
from jax.experimental.pallas import tpu as pltpu
from jax.sharding import PartitionSpec as P

MESH = pl.DeviceIdType.MESH
F32 = jnp.float32
BF16 = jnp.bfloat16
DIRS = [(dx, dy) for dx in (-1, 0, 1) for dy in (-1, 0, 1) if (dx, dy) != (0, 0)]
NEAR = [(dx, dy) for dx in (-1, 0, 1) for dy in (-1, 0, 1)]
FAR = [(dx, dy) for dx in range(-3, 4) for dy in range(-3, 4) if max(abs(dx), abs(dy)) >= 2]
OFF1, OFF2, OFF3, OFF4, OFF5, ROWS = 512, 640, 672, 704, 736, 768


def nt(a, b):
    return lax.dot_general(a, b, (((1,), (1,)), ((), ())), preferred_element_type=F32)


def nn(a, b):
    return jnp.dot(a, b, preferred_element_type=F32)


def edge(step, size, width):
    if step == 0:
        return pl.ds(width, size), pl.ds(width, size)
    if step > 0:
        return pl.ds(size, width), pl.ds(0, width)
    return pl.ds(width, width), pl.ds(size + width, width)


def kernel(
    n_rows,
    n_cols,
    exc_hbm,
    area_hbm,
    cond_hbm,
    nb_hbm,
    mask_hbm,
    sm_hbm,
    te_hbm,
    tr_hbm,
    su_hbm,
    pot_ref,
    adj_ref,
    epad,
    area_v,
    cond_v,
    nb_v,
    sm_v,
    te_v,
    tr_v,
    su_v,
    wts,
    leaf,
    l1,
    l2,
    l3,
    l4,
    l5,
    mask_ref,
    nf,
    acc,
    ret_row,
    ret_col,
    in_row,
    in_col,
    wt,
    gain,
    sel5,
    sel4,
    sel3,
    loc2,
    loc1,
    locl,
    in_sem,
    map_sem,
    nb_sem,
    hs_sem,
    hr_sem,
    s3_sem,
    r3_sem,
    sp_sem,
    rp_sem,
    s4_sem,
    r4_sem,
):
    r = lax.axis_index("bx")
    c = lax.axis_index("by")
    r2, c2 = r // 2, c // 2
    r4, c4 = r // 4, c // 4

    cp_exc = pltpu.make_async_copy(exc_hbm, epad.at[1:9, 1:9], in_sem.at[0])
    cp_area = pltpu.make_async_copy(area_hbm, area_v, in_sem.at[1])
    cp_cond = pltpu.make_async_copy(cond_hbm, cond_v, in_sem.at[2])
    cp_su = pltpu.make_async_copy(su_hbm, su_v, in_sem.at[3])
    cp_mask = pltpu.make_async_copy(mask_hbm, mask_ref, in_sem.at[5])
    cp_tr = pltpu.make_async_copy(tr_hbm, tr_v, in_sem.at[4])

    def cp_sm(x):
        return pltpu.make_async_copy(sm_hbm.at[x], sm_v.at[x], map_sem.at[0, x])

    def cp_te(x):
        return pltpu.make_async_copy(te_hbm.at[x], te_v.at[x], map_sem.at[1, x])

    def cp_nb(x):
        return pltpu.make_async_copy(nb_hbm.at[x], nb_v.at[x], nb_sem.at[x])

    cp_exc.start()
    cp_area.start()
    cp_cond.start()
    for x in range(8):
        cp_sm(x).start()
        cp_te(x).start()
    cp_su.start()
    cp_tr.start()
    cp_mask.start()
    for x in range(8):
        cp_nb(x).start()

    def clear(ref, rows, cols, width, wide):
        ref[0:width] = jnp.zeros((width,) + ref.shape[1:], ref.dtype)
        ref[rows + width :] = jnp.zeros((width,) + ref.shape[1:], ref.dtype)
        side = jnp.zeros((rows, wide) + ref.shape[2:], ref.dtype)
        ref[width : rows + width, 0:wide] = side
        ref[width : rows + width, cols + wide :] = side

    clear(epad, 8, 8, 1, 1)
    clear(leaf, 8, 4, 2, 1)
    clear(l1, 4, 2, 2, 1)
    clear(l2, 2, 1, 2, 1)
    for ref in (l3, l4, l5, in_row, in_col):
        ref[...] = jnp.zeros(ref.shape, ref.dtype)

    def inside(row, col):
        return (row >= 0) & (row < n_rows) & (col >= 0) & (col < n_cols)

    def row_peers():
        return [(row, row != r) for row in range(n_rows)]

    def pair_peers():
        return [(v, 2 * v + c % 2, v != c2) for v in range(n_cols // 2)]

    barrier = pltpu.get_barrier_semaphore()
    greeted = jnp.int32(0)

    def greet(row, col, present):
        @pl.when(present)
        def _():
            pl.semaphore_signal(barrier, inc=1, device_id=(row, col), device_id_type=MESH)

        return present.astype(jnp.int32)

    for dy in (-1, 1):
        greeted = greeted + greet(r, c + dy, inside(r, c + dy))
    for row, present in row_peers():
        greeted = greeted + greet(jnp.int32(row), c, present)
    for _, col, present in pair_peers():
        greeted = greeted + greet(r, col, present)
    pl.semaphore_wait(barrier, greeted)

    def halo_copy(number, direction):
        dx, dy = DIRS[direction]
        if number == 4:
            place = 0 if dx + dy > 0 else 1
            src, dst = (ret_row, in_row) if dy == 0 else (ret_col, in_col)
            src, dst = src.at[place], dst.at[place]
        else:
            ref, rows, width, cols, wide = (
                (epad, 8, 1, 8, 1),
                (leaf, 8, 2, 4, 1),
                (l1, 4, 2, 2, 1),
                (l2, 2, 2, 1, 1),
            )[number]
            src_rows, dst_rows = edge(dx, rows, width)
            src_cols, dst_cols = edge(dy, cols, wide)
            src = ref.at[src_rows if dy == 0 or dx == 0 else dst_rows, src_cols]
            dst = ref.at[dst_rows, dst_cols]
        return pltpu.make_async_remote_copy(
            src_ref=src,
            dst_ref=dst,
            send_sem=hs_sem.at[number, direction],
            recv_sem=hr_sem.at[number, direction],
            device_id=(r + dx, c) if dy == 0 else (r, c + dy),
            device_id_type=MESH,
        )

    ROW = [i for i, (dx, dy) in enumerate(DIRS) if dy == 0]
    COL = [i for i, (dx, dy) in enumerate(DIRS) if dx == 0]
    CORNER = [i for i, (dx, dy) in enumerate(DIRS) if dx * dy != 0]

    def leaves(direction):
        dx, dy = DIRS[direction]
        if dy == 0:
            return inside(r + dx, c)
        return inside(r - dx, c) & inside(r, c + dy)

    def halo_start(number, directions):
        for direction in directions:

            @pl.when(leaves(direction))
            def _():
                halo_copy(number, direction).start()

    def halo_received(number, directions):
        for direction in directions:
            dx, dy = DIRS[direction]

            @pl.when(inside(r - dx, c - dy))
            def _():
                halo_copy(number, direction).wait_recv()

    def halo_sent(number, directions):
        for direction in directions:

            @pl.when(leaves(direction))
            def _():
                halo_copy(number, direction).wait_send()

    def l3_row_copy(row, sender):
        return pltpu.make_async_remote_copy(
            src_ref=l3.at[2 + c % 2, sender + 2],
            dst_ref=l3.at[2 + c % 2, sender + 2],
            send_sem=s3_sem.at[row],
            recv_sem=r3_sem.at[sender],
            device_id=(jnp.int32(row), c),
            device_id_type=MESH,
        )

    other = c + 1 - 2 * (c % 2)

    def l3_col_copy(step, received=False):
        rows = pl.ds(2, n_rows) if step == 0 else pl.ds(2 * r2, 6)
        own = 2 + c % 2
        there = 2 + (1 - c % 2) if received else own
        if step == 0:
            src, dst, col = own, there, other
        elif step == 1:
            src, dst, col = own, c % 2, c + 2
        elif step == 2:
            src, dst, col = own, 4 + c % 2, c - 2
        else:
            src = c % 2 + (0 if step == 3 else 4)
            dst = (1 - c % 2 if received else c % 2) + (0 if step == 3 else 4)
            col = other
        return pltpu.make_async_remote_copy(
            src_ref=l3.at[src, rows],
            dst_ref=l3.at[dst, rows],
            send_sem=sp_sem.at[step],
            recv_sem=rp_sem.at[step],
            device_id=(r, col),
            device_id_type=MESH,
        )

    has_last, has_next = c2 > 0, c2 < n_cols // 2 - 1
    COL_SENDS = (True, has_next, has_last, has_last, has_next)
    COL_COMES = (True, has_last, has_next, has_last, has_next)

    part = n_rows // 4

    quarter = n_cols // 4
    mirror = (c2 + quarter) % (2 * quarter)
    ring = [quarter * (c2 // quarter) + (c2 + k) % quarter for k in range(1, quarter)]

    def l4_copy(to, owner, slot):
        place = l4.at[owner + 2, pl.ds(2 + part * (c % 2), part)]
        return pltpu.make_async_remote_copy(
            src_ref=place,
            dst_ref=place,
            send_sem=s4_sem.at[slot],
            recv_sem=r4_sem.at[owner],
            device_id=(r, 2 * to + c % 2),
            device_id_type=MESH,
        )

    def mirrored(v):
        return (v + quarter) % (2 * quarter)

    def l4_pass(half):
        place = l4.at[pl.ds(2, n_cols // 2), pl.ds(2 + part * half, part)]
        return pltpu.make_async_remote_copy(
            src_ref=place,
            dst_ref=place,
            send_sem=sp_sem.at[5],
            recv_sem=rp_sem.at[5],
            device_id=(r, other),
            device_id_type=MESH,
        )

    def l3_col_start(step):
        @pl.when(COL_SENDS[step])
        def _():
            l3_col_copy(step).start()

    def l3_col_received(step):
        @pl.when(COL_COMES[step])
        def _():
            l3_col_copy(step, True).wait_recv()

    cp_exc.wait()
    halo_start(0, ROW + COL)
    acc[...] = jnp.zeros(acc.shape, F32)
    cp_area.wait()
    cp_cond.wait()

    labels = lax.broadcasted_iota(jnp.int32, (32, 128), 0)

    def moments(x, carry):
        cp_sm(x).wait()
        cp_te(x).wait()
        conds = cond_v[x]
        areas = area_v[x].astype(F32)
        for y in range(8):
            half = slice((y % 2) * 128, (y % 2) * 128 + 128)
            chosen = labels == conds[y : y + 1]
            w = jnp.where(chosen, areas[y : y + 1], 0.0).astype(BF16)
            wts[x, y] = w
            leaf[x + 2, 1 + y // 2, 0, :, half] = nt(epad[x + 1, y + 1], sm_v[x, y]).astype(BF16)
            leaf[x + 2, 1 + y // 2, 1, :, half] = nn(w, te_v[x, y]).astype(BF16)
        return carry

    lax.fori_loop(0, 8, moments, 0)

    cp_su.wait()
    ups = [jnp.concatenate([su_v[a, 0], su_v[a, 1]], axis=1) for a in range(2)]

    for u in range(4):
        total = sum(nt(leaf[2 * u + a + 2, 1:5].reshape(256, 256), ups[a]) for a in range(2))
        made = total.astype(BF16).reshape(4, 2, 32, 128)
        for v in range(4):
            l1[u + 2, 1 + v // 2, :, :, (v % 2) * 128 : (v % 2) * 128 + 128] = made[v]
    total = sum(
        nt(jnp.concatenate([l1[2 * u + a + 2, 1:3].reshape(128, 256) for u in range(2)]), ups[a])
        for a in range(2)
    )
    made = total.astype(BF16).reshape(2, 2, 2, 32, 128)
    for u in range(2):
        for v in range(2):
            l2[u + 2, 1, :, :, v * 128 : v * 128 + 128] = made[u, v]
    total = sum(nt(l2[a + 2, 1].reshape(64, 256), ups[a]) for a in range(2))
    l3[2 + c % 2, r + 2] = total.astype(BF16).reshape(2, 32, 128)

    for row, present in row_peers():

        @pl.when(present)
        def _():
            l3_row_copy(row, r).start()

    for number in (1, 2, 3):
        halo_start(number, ROW)
    halo_received(0, ROW)
    halo_start(0, CORNER)
    for number in (3, 2):
        halo_start(number, COL)

    cp_tr.wait()
    for dx in range(-3, 4):
        for dy in range(-1, 2):
            for i in range(2):
                for j in range(2):
                    offset = (dx, 2 * dy + j - i)
                    block = (
                        tr_v[FAR.index(offset)] if offset in FAR else jnp.zeros((128, 128), BF16)
                    )
                    wt[
                        3 * (dx + 3) + dy + 1,
                        i * 128 : i * 128 + 128,
                        j * 128 : j * 128 + 128,
                    ] = block

    halo_received(0, COL + CORNER)
    cp_mask.wait()

    def near(x, carry):
        cp_nb(x).wait()
        for y in range(8):
            blocks = jnp.concatenate([nb_v[x, y, k] for k in range(9)], axis=1)
            keep = [mask_ref[x, y, k].astype(F32) for k in range(9)]
            source = jnp.concatenate(
                [
                    (epad[x + 1 + dx, y + 1 + dy].astype(F32) * keep[k]).astype(BF16)
                    for k, (dx, dy) in enumerate(NEAR)
                ],
                axis=1,
            )
            nf[x, y] = nt(source, blocks)
            back = nn(wts[x, y], blocks)
            for k, (dx, dy) in enumerate(NEAR):
                acc[x + 1 + dx, y + 1 + dy] += keep[k] * back[:, k * 128 : k * 128 + 128]
        return carry

    lax.fori_loop(0, 2, near, 0)

    for row, present in row_peers():

        @pl.when(present)
        def _():
            l3_row_copy(row, jnp.int32(row)).wait_recv()

    for step in range(3):
        l3_col_start(step)

    lax.fori_loop(2, 4, near, 0)

    l3_col_received(0)

    def up_strip(ref, col, first, rows):
        total = 0.0
        for a in range(2):
            pairs = [
                jnp.concatenate(
                    [
                        ref[col, first + 2 * u + a].reshape(64, 128),
                        ref[col + 1, first + 2 * u + a].reshape(64, 128),
                    ],
                    axis=1,
                )
                for u in range(rows)
            ]
            total = total + nt(jnp.concatenate(pairs, axis=0), ups[a])
        return total.astype(BF16).reshape(rows, 2, 32, 128)

    l4[c2 + 2, pl.ds(2 + part * (c % 2), part)] = up_strip(l3, 2, 2 + 2 * part * (c % 2), part)
    l4_copy(mirror, c2, mirror).start()
    for v in ring:
        l4_copy(v, c2, v).start()

    for number in (1,):
        halo_start(number, COL)

    lax.fori_loop(4, 6, near, 0)

    l4_copy(mirror, mirror, mirror).wait_recv()
    for v in ring:
        l4_copy(v, mirror, mirrored(v)).start()
    l3_col_received(1)
    l3_col_start(3)
    l3_col_received(2)
    l3_col_start(4)
    pass

    lax.fori_loop(6, 8, near, 0)

    for place, row in ((0, 9), (1, 0)):
        ret_row[place] = acc[row].astype(BF16)
    halo_start(4, ROW)

    halo_received(1, ROW)
    halo_start(1, CORNER)
    halo_received(1, COL)

    INNER, OUTER, COARSE = (1, 2), (0, 3), ()

    def sources(group, side, a, dx, dy):
        parts = []
        for i in group:
            parts.append(leaf[2 * i + a + dx + 2, 1 + dy : 5 + dy, side].reshape(128, 256))
        if group:
            return jnp.concatenate(parts, axis=0)
        for i in range(2):
            parts.append(l1[2 * i + a + dx + 2, 1 + dy : 3 + dy, side].reshape(64, 256))
        parts.append(l2[a + dx + 2, 1 + dy, side])
        for ref, row, col in (
            (l3, 2 * r2, 0),
            (l4, 2 * r4, 2 * c4),
            (l5, 0, 2 * (c // 8)),
        ):
            row = row + a + dx + 2
            col = col + 2 * (1 + dy)
            parts.append(jnp.concatenate([ref[col, row, side], ref[col + 1, row, side]], axis=1))
        return jnp.concatenate(parts, axis=0)

    def interact(group, side, a):
        offsets = [
            (dx, dy)
            for dx in range(-2 - a, 4 - a)
            for dy in (-1, 0, 1)
            if abs(dx) >= 2 or dy != 0
        ]
        total = 0.0
        for dx, dy in offsets:
            taken = sources(group, side, a, dx, dy)
            if side == 0:
                total = total + nt(taken, wt[3 * (dx + 3) + dy + 1])
            else:
                total = total + nn(taken, wt[3 * (3 - dx) + 1 - dy])
        return total

    def inner_rows():
        for side in range(2):
            for a in range(2):
                gain[side, a, 128:384] = interact(INNER, side, a)

    inner_rows()
    for v in ring:
        l4_copy(v, v, v).wait_recv()
        l4_copy(v, mirrored(v), mirrored(v)).wait_recv()

    l4_pass(c % 2).start()
    halo_received(2, ROW)
    halo_start(2, CORNER)
    halo_received(3, ROW)
    halo_start(3, CORNER)
    halo_received(4, ROW)
    for place, row in ((0, 1), (1, 8)):
        acc[row] += in_row[place].astype(F32)
    for place, col in ((0, 9), (1, 0)):
        ret_col[place] = acc[1:9, col].astype(BF16)
    halo_start(4, COL)
    halo_received(1, CORNER)
    for side in range(2):
        for a in range(2):
            made = interact(OUTER, side, a)
            gain[side, a, 0:128] = made[0:128]
            gain[side, a, 384:OFF1] = made[128:256]

    pass
    l3_col_received(3)
    l3_col_received(4)
    l4_pass(1 - c % 2).wait_recv()
    for col in range(n_cols // 4):
        l5[col + 2, 2 : 2 + n_rows // 4] = up_strip(l4, 2 + 2 * col, 2, n_rows // 4)
    for number in (2, 3):
        halo_received(number, COL + CORNER)

    for side in range(2):
        for a in range(2):
            gain[side, a, OFF1:ROWS] = interact(COARSE, side, a)

    for a in range(2):
        for side in range(2):
            top = gain[side, a, OFF5 : OFF5 + 32].astype(BF16)
            for b in range(2):
                sel5[a, b, side] = top[:, b * 128 : b * 128 + 128]
    parent = sel5[r4, c4 % 2].reshape(64, 128)
    for off, sel, row, col in (
        (OFF4, sel4, r2 % 2, c2 % 2),
        (OFF3, sel3, r % 2, c % 2),
        (OFF2, loc2, None, None),
    ):
        for a in range(2):
            spread = nn(parent, ups[a])
            for side in range(2):
                made = spread[side * 32 : side * 32 + 32] + gain[side, a, off : off + 32]
                made = made.astype(BF16)
                for b in range(2):
                    sel[a, b, side] = made[:, b * 128 : b * 128 + 128]
        if row is not None:
            parent = sel[row, col].reshape(64, 128)

    for upper, lower, count, off in ((loc2, loc1, 2, OFF1), (loc1, locl, 4, 0)):
        for u in range(count):
            for a in range(2):
                spread = nn(upper[u].reshape(count * 64, 128), ups[a])
                for v in range(count):
                    for side in range(2):
                        first = v * 64 + side * 32
                        at = off + (u * count + v) * 32
                        made = spread[first : first + 32] + gain[side, a, at : at + 32]
                        made = made.astype(BF16)
                        for b in range(2):
                            lower[2 * u + a, 2 * v + b, side] = made[:, b * 128 : b * 128 + 128]

    halo_received(4, COL)
    for place, col in ((0, 1), (1, 8)):
        acc[1:9, col] += in_col[place].astype(F32)

    def finish(x, carry):
        for y in range(8):
            pot_ref[x, y] = (nf[x, y] + nt(locl[x, y, 0], te_v[x, y])).astype(BF16)
            adj_ref[x, y] = (acc[x + 1, y + 1] + nn(locl[x, y, 1], sm_v[x, y])).astype(BF16)
        return carry

    lax.fori_loop(0, 8, finish, 0)

    for number in range(5):
        halo_sent(number, ROW + COL + (CORNER if number < 4 else []))
    for row, present in row_peers():

        @pl.when(present)
        def _():
            l3_row_copy(row, r).wait_send()

    for step in range(5):

        @pl.when(COL_SENDS[step])
        def _():
            l3_col_copy(step).wait_send()

    l4_pass(c % 2).wait_send()
    l4_copy(mirror, c2, mirror).wait_send()
    for v in ring:
        l4_copy(v, c2, v).wait_send()
        l4_copy(v, mirror, mirrored(v)).wait_send()


def solution(mesh):
    n_rows, n_cols = mesh.shape["bx"], mesh.shape["by"]
    hbm = pl.BlockSpec(memory_space=pl.ANY)
    vmem = pl.BlockSpec(memory_space=pltpu.VMEM)
    box = (2, 32, 128)
    pair = (2, 32, 256)
    scratch = [
        pltpu.VMEM((10, 10, 32, 128), BF16),
        pltpu.VMEM((8, 8, 128), BF16),
        pltpu.VMEM((8, 8, 128), jnp.int32),
        pltpu.VMEM((8, 8, 9, 128, 128), BF16),
        pltpu.VMEM((8, 8, 128, 128), BF16),
        pltpu.VMEM((8, 8, 128, 128), BF16),
        pltpu.VMEM((40, 128, 128), BF16),
        pltpu.VMEM((2, 2, 128, 128), BF16),
        pltpu.VMEM((8, 8, 32, 128), BF16),
        pltpu.VMEM((12, 6) + pair, BF16),
        pltpu.VMEM((8, 4) + pair, BF16),
        pltpu.VMEM((6, 3) + pair, BF16),
        pltpu.VMEM((6, n_rows + 4) + box, BF16),
        pltpu.VMEM((n_cols // 2 + 4, n_rows // 2 + 4) + box, BF16),
        pltpu.VMEM((n_cols // 4 + 4, n_rows // 4 + 4) + box, BF16),
        pltpu.SMEM((8, 8, 9), jnp.int32),
        pltpu.VMEM((8, 8, 32, 128), F32),
        pltpu.VMEM((10, 10, 32, 128), F32),
        pltpu.VMEM((2, 10, 32, 128), BF16),
        pltpu.VMEM((2, 8, 32, 128), BF16),
        pltpu.VMEM((2, 10, 32, 128), BF16),
        pltpu.VMEM((2, 8, 32, 128), BF16),
        pltpu.VMEM((21, 256, 256), BF16),
        pltpu.VMEM((2, 2, ROWS, 256), F32),
        pltpu.VMEM((2, 2) + box, BF16),
        pltpu.VMEM((2, 2) + box, BF16),
        pltpu.VMEM((2, 2) + box, BF16),
        pltpu.VMEM((2, 2) + box, BF16),
        pltpu.VMEM((4, 4) + box, BF16),
        pltpu.VMEM((8, 8) + box, BF16),
        pltpu.SemaphoreType.DMA((6,)),
        pltpu.SemaphoreType.DMA((2, 8)),
        pltpu.SemaphoreType.DMA((8,)),
        pltpu.SemaphoreType.DMA((5, 8)),
        pltpu.SemaphoreType.DMA((5, 8)),
        pltpu.SemaphoreType.DMA((n_rows,)),
        pltpu.SemaphoreType.DMA((n_rows,)),
        pltpu.SemaphoreType.DMA((6,)),
        pltpu.SemaphoreType.DMA((6,)),
        pltpu.SemaphoreType.DMA((n_cols // 2,)),
        pltpu.SemaphoreType.DMA((n_cols // 2,)),
    ]

    def per_device(*arrays):
        def body(*refs):
            kernel(n_rows, n_cols, *refs)

        kept = pltpu.VMEM(arrays[0].shape, BF16)
        return pl.pallas_call(
            body,
            out_shape=(kept, kept),
            in_specs=[hbm, hbm, hbm, hbm, hbm, hbm, hbm, hbm, hbm],
            out_specs=(vmem, vmem),
            scratch_shapes=scratch,
            compiler_params=pltpu.CompilerParams(
                collective_id=0, has_side_effects=True, vmem_limit_bytes=56 * 1024 * 1024
            ),
            cost_estimate=pl.CostEstimate(
                flops=4300000000, bytes_accessed=26000000, transcendentals=0
            ),
            name="fmm",
        )(*arrays)

    placed = (
        P("bx", "by", None, None),
        P("bx", "by", None),
        P("bx", "by", None),
        P("bx", "by", None, None, None),
        P("bx", "by", None),
        P("bx", "by", None, None),
        P("bx", "by", None, None),
        P(),
        P(),
    )
    return jax.shard_map(
        per_device,
        mesh=mesh,
        in_specs=placed,
        out_specs=(P("bx", "by", None, None), P("bx", "by", None, None)),
        check_vma=False,
    )
```

```python
import jax
import jax.numpy as jnp
from jax import lax
from jax.experimental import pallas as pl
from jax.experimental.pallas import tpu as pltpu
from jax.sharding import PartitionSpec as P

MESH = pl.DeviceIdType.MESH
F32 = jnp.float32
BF16 = jnp.bfloat16
DIRS = [(dx, dy) for dx in (-1, 0, 1) for dy in (-1, 0, 1) if (dx, dy) != (0, 0)]
NEAR = [(dx, dy) for dx in (-1, 0, 1) for dy in (-1, 0, 1)]
FAR = [(dx, dy) for dx in range(-3, 4) for dy in range(-3, 4) if max(abs(dx), abs(dy)) >= 2]
OFF1, OFF2, OFF3, OFF4, OFF5, ROWS = 512, 640, 672, 704, 736, 768


def nt(a, b):
    return lax.dot_general(a, b, (((1,), (1,)), ((), ())), preferred_element_type=F32)


def nn(a, b):
    return jnp.dot(a, b, preferred_element_type=F32)


def edge(step, size, width):
    if step == 0:
        return pl.ds(width, size), pl.ds(width, size)
    if step > 0:
        return pl.ds(size, width), pl.ds(0, width)
    return pl.ds(width, width), pl.ds(size + width, width)


def kernel(
    n_rows,
    n_cols,
    exc_hbm,
    area_hbm,
    cond_hbm,
    nb_hbm,
    mask_hbm,
    sm_hbm,
    te_hbm,
    tr_hbm,
    su_hbm,
    pot_ref,
    adj_ref,
    epad,
    area_v,
    cond_v,
    nb_v,
    sm_v,
    te_v,
    tr_v,
    su_v,
    wts,
    leaf,
    l1,
    l2,
    l3,
    l4,
    l5,
    mask_ref,
    nf,
    acc,
    ret_row,
    ret_col,
    in_row,
    in_col,
    wt,
    gain,
    sel5,
    sel4,
    sel3,
    loc2,
    loc1,
    locl,
    in_sem,
    map_sem,
    nb_sem,
    hs_sem,
    hr_sem,
    s3_sem,
    r3_sem,
    sp_sem,
    rp_sem,
    s4_sem,
    r4_sem,
):
    r = lax.axis_index("bx")
    c = lax.axis_index("by")
    r2, c2 = r // 2, c // 2
    r4, c4 = r // 4, c // 4

    cp_exc = pltpu.make_async_copy(exc_hbm, epad.at[1:9, 1:9], in_sem.at[0])
    cp_area = pltpu.make_async_copy(area_hbm, area_v, in_sem.at[1])
    cp_cond = pltpu.make_async_copy(cond_hbm, cond_v, in_sem.at[2])
    cp_su = pltpu.make_async_copy(su_hbm, su_v, in_sem.at[3])
    cp_mask = pltpu.make_async_copy(mask_hbm, mask_ref, in_sem.at[5])
    cp_tr = pltpu.make_async_copy(tr_hbm, tr_v, in_sem.at[4])

    def cp_sm(x):
        return pltpu.make_async_copy(sm_hbm.at[x], sm_v.at[x], map_sem.at[0, x])

    def cp_te(x):
        return pltpu.make_async_copy(te_hbm.at[x], te_v.at[x], map_sem.at[1, x])

    def cp_nb(x):
        return pltpu.make_async_copy(nb_hbm.at[x], nb_v.at[x], nb_sem.at[x])

    cp_exc.start()
    cp_area.start()
    cp_cond.start()
    for x in range(8):
        cp_sm(x).start()
        cp_te(x).start()
    cp_su.start()
    cp_tr.start()
    cp_mask.start()
    for x in range(8):
        cp_nb(x).start()

    def clear(ref, rows, cols, width, wide):
        ref[0:width] = jnp.zeros((width,) + ref.shape[1:], ref.dtype)
        ref[rows + width :] = jnp.zeros((width,) + ref.shape[1:], ref.dtype)
        side = jnp.zeros((rows, wide) + ref.shape[2:], ref.dtype)
        ref[width : rows + width, 0:wide] = side
        ref[width : rows + width, cols + wide :] = side

    clear(epad, 8, 8, 1, 1)
    clear(leaf, 8, 4, 2, 1)
    clear(l1, 4, 2, 2, 1)
    clear(l2, 2, 1, 2, 1)
    for ref in (l3, l4, l5, in_row, in_col):
        ref[...] = jnp.zeros(ref.shape, ref.dtype)

    def inside(row, col):
        return (row >= 0) & (row < n_rows) & (col >= 0) & (col < n_cols)

    def row_peers():
        return [(row, row != r) for row in range(n_rows)]

    def pair_peers():
        return [(v, 2 * v + c % 2, v != c2) for v in range(n_cols // 2)]

    barrier = pltpu.get_barrier_semaphore()
    greeted = jnp.int32(0)

    def greet(row, col, present):
        @pl.when(present)
        def _():
            pl.semaphore_signal(barrier, inc=1, device_id=(row, col), device_id_type=MESH)

        return present.astype(jnp.int32)

    for dy in (-1, 1):
        greeted = greeted + greet(r, c + dy, inside(r, c + dy))
    for row, present in row_peers():
        greeted = greeted + greet(jnp.int32(row), c, present)
    for _, col, present in pair_peers():
        greeted = greeted + greet(r, col, present)
    pl.semaphore_wait(barrier, greeted)

    def halo_copy(number, direction):
        dx, dy = DIRS[direction]
        if number == 4:
            place = 0 if dx + dy > 0 else 1
            src, dst = (ret_row, in_row) if dy == 0 else (ret_col, in_col)
            src, dst = src.at[place], dst.at[place]
        else:
            ref, rows, width, cols, wide = (
                (epad, 8, 1, 8, 1),
                (leaf, 8, 2, 4, 1),
                (l1, 4, 2, 2, 1),
                (l2, 2, 2, 1, 1),
            )[number]
            src_rows, dst_rows = edge(dx, rows, width)
            src_cols, dst_cols = edge(dy, cols, wide)
            if number < 2 or dx * dy != 0:
                src = ref.at[src_rows if dy == 0 or dx == 0 else dst_rows, src_cols]
                dst = ref.at[dst_rows, dst_cols]
            elif dy == 0:
                src = ref.at[rows if dx > 0 else 3, 1 : cols + 1]
                dst = ref.at[0 if dx > 0 else rows + 3, 1 : cols + 1]
            else:
                lanes = slice(0, 128) if dy > 0 else slice(128, 256)
                src = ref.at[src_rows, cols if dy > 0 else 1, :, :, lanes]
                dst = ref.at[dst_rows, 0 if dy > 0 else cols + 1, :, :, lanes]
        return pltpu.make_async_remote_copy(
            src_ref=src,
            dst_ref=dst,
            send_sem=hs_sem.at[number, direction],
            recv_sem=hr_sem.at[number, direction],
            device_id=(r + dx, c) if dy == 0 else (r, c + dy),
            device_id_type=MESH,
        )

    ROW = [i for i, (dx, dy) in enumerate(DIRS) if dy == 0]
    COL = [i for i, (dx, dy) in enumerate(DIRS) if dx == 0]
    CORNER = [i for i, (dx, dy) in enumerate(DIRS) if dx * dy != 0]

    def leaves(direction):
        dx, dy = DIRS[direction]
        if dy == 0:
            return inside(r + dx, c)
        return inside(r - dx, c) & inside(r, c + dy)

    def halo_start(number, directions):
        for direction in directions:

            @pl.when(leaves(direction))
            def _():
                halo_copy(number, direction).start()

    def halo_received(number, directions):
        for direction in directions:
            dx, dy = DIRS[direction]

            @pl.when(inside(r - dx, c - dy))
            def _():
                halo_copy(number, direction).wait_recv()

    def halo_sent(number, directions):
        for direction in directions:

            @pl.when(leaves(direction))
            def _():
                halo_copy(number, direction).wait_send()

    def l3_row_copy(row, sender):
        return pltpu.make_async_remote_copy(
            src_ref=l3.at[2 + c % 2, sender + 2],
            dst_ref=l3.at[2 + c % 2, sender + 2],
            send_sem=s3_sem.at[row],
            recv_sem=r3_sem.at[sender],
            device_id=(jnp.int32(row), c),
            device_id_type=MESH,
        )

    other = c + 1 - 2 * (c % 2)

    def l3_col_copy(step, received=False):
        rows = pl.ds(2, n_rows) if step == 0 else pl.ds(2 * r2, 6)
        own = 2 + c % 2
        there = 2 + (1 - c % 2) if received else own
        if step == 0:
            src, dst, col = own, there, other
        elif step == 1:
            src, dst, col = own, c % 2, c + 2
        elif step == 2:
            src, dst, col = own, 4 + c % 2, c - 2
        else:
            src = c % 2 + (0 if step == 3 else 4)
            dst = (1 - c % 2 if received else c % 2) + (0 if step == 3 else 4)
            col = other
        return pltpu.make_async_remote_copy(
            src_ref=l3.at[src, rows],
            dst_ref=l3.at[dst, rows],
            send_sem=sp_sem.at[step],
            recv_sem=rp_sem.at[step],
            device_id=(r, col),
            device_id_type=MESH,
        )

    has_last, has_next = c2 > 0, c2 < n_cols // 2 - 1
    COL_SENDS = (True, has_next, has_last, has_last, has_next)
    COL_COMES = (True, has_last, has_next, has_last, has_next)

    part = n_rows // 4

    quarter = n_cols // 4
    mirror = (c2 + quarter) % (2 * quarter)
    ring = [quarter * (c2 // quarter) + (c2 + k) % quarter for k in range(1, quarter)]

    def l4_copy(to, owner, slot):
        place = l4.at[owner + 2, pl.ds(2 + part * (c % 2), part)]
        return pltpu.make_async_remote_copy(
            src_ref=place,
            dst_ref=place,
            send_sem=s4_sem.at[slot],
            recv_sem=r4_sem.at[owner],
            device_id=(r, 2 * to + c % 2),
            device_id_type=MESH,
        )

    def mirrored(v):
        return (v + quarter) % (2 * quarter)

    def l4_pass(half):
        place = l4.at[pl.ds(2, n_cols // 2), pl.ds(2 + part * half, part)]
        return pltpu.make_async_remote_copy(
            src_ref=place,
            dst_ref=place,
            send_sem=sp_sem.at[5],
            recv_sem=rp_sem.at[5],
            device_id=(r, other),
            device_id_type=MESH,
        )

    def l3_col_start(step):
        @pl.when(COL_SENDS[step])
        def _():
            l3_col_copy(step).start()

    def l3_col_received(step):
        @pl.when(COL_COMES[step])
        def _():
            l3_col_copy(step, True).wait_recv()

    cp_exc.wait()
    halo_start(0, ROW + COL)
    acc[...] = jnp.zeros(acc.shape, F32)
    cp_area.wait()
    cp_cond.wait()

    labels = lax.broadcasted_iota(jnp.int32, (32, 128), 0)

    def moments(x, carry):
        cp_sm(x).wait()
        cp_te(x).wait()
        conds = cond_v[x]
        areas = area_v[x].astype(F32)
        for y in range(8):
            half = slice((y % 2) * 128, (y % 2) * 128 + 128)
            chosen = labels == conds[y : y + 1]
            w = jnp.where(chosen, areas[y : y + 1], 0.0).astype(BF16)
            wts[x, y] = w
            leaf[x + 2, 1 + y // 2, 0, :, half] = nt(epad[x + 1, y + 1], sm_v[x, y]).astype(BF16)
            leaf[x + 2, 1 + y // 2, 1, :, half] = nn(w, te_v[x, y]).astype(BF16)
        return carry

    lax.fori_loop(0, 8, moments, 0)

    cp_su.wait()
    ups = [jnp.concatenate([su_v[a, 0], su_v[a, 1]], axis=1) for a in range(2)]

    def ring_rows(lower, upper, rows, cols):
        total = sum(
            nt(
                jnp.concatenate(
                    [lower[low + a, 1 : cols + 1].reshape(cols * 64, 256) for low in (0, 2 * rows + 2)],
                    axis=0,
                ),
                ups[a],
            )
            for a in range(2)
        )
        made = total.astype(BF16).reshape(2, cols, 2, 32, 128)
        for place, row in ((0, 1), (1, rows + 2)):
            for v in range(cols):
                upper[row, 1 + v // 2, :, :, (v % 2) * 128 : (v % 2) * 128 + 128] = made[place, v]

    def ring_cols(lower, upper, rows, cols):
        total = sum(
            nt(
                jnp.concatenate(
                    [
                        lower[2 * u + a + 2, col].reshape(64, 256)
                        for col in (0, cols + 1)
                        for u in range(rows)
                    ],
                    axis=0,
                ),
                ups[a],
            )
            for a in range(2)
        )
        made = total.astype(BF16).reshape(2, rows, 2, 32, 128)
        upper[2 : rows + 2, 0, :, :, 128:256] = made[0]
        upper[2 : rows + 2, cols // 2 + 1, :, :, 0:128] = made[1]

    for u in range(4):
        total = sum(nt(leaf[2 * u + a + 2, 1:5].reshape(256, 256), ups[a]) for a in range(2))
        made = total.astype(BF16).reshape(4, 2, 32, 128)
        for v in range(4):
            l1[u + 2, 1 + v // 2, :, :, (v % 2) * 128 : (v % 2) * 128 + 128] = made[v]
    total = sum(
        nt(jnp.concatenate([l1[2 * u + a + 2, 1:3].reshape(128, 256) for u in range(2)]), ups[a])
        for a in range(2)
    )
    made = total.astype(BF16).reshape(2, 2, 2, 32, 128)
    for u in range(2):
        for v in range(2):
            l2[u + 2, 1, :, :, v * 128 : v * 128 + 128] = made[u, v]
    total = sum(nt(l2[a + 2, 1].reshape(64, 256), ups[a]) for a in range(2))
    l3[2 + c % 2, r + 2] = total.astype(BF16).reshape(2, 32, 128)

    for row, present in row_peers():

        @pl.when(present)
        def _():
            l3_row_copy(row, r).start()

    for number in (1, 2, 3):
        halo_start(number, ROW)
    halo_received(0, ROW)
    halo_start(0, CORNER)
    for number in (1,):
        halo_start(number, COL)

    cp_tr.wait()
    for dx in range(-3, 4):
        for dy in range(-1, 2):
            for i in range(2):
                for j in range(2):
                    offset = (dx, 2 * dy + j - i)
                    block = (
                        tr_v[FAR.index(offset)] if offset in FAR else jnp.zeros((128, 128), BF16)
                    )
                    wt[
                        3 * (dx + 3) + dy + 1,
                        i * 128 : i * 128 + 128,
                        j * 128 : j * 128 + 128,
                    ] = block

    halo_received(0, COL + CORNER)
    cp_mask.wait()

    def near(x, carry):
        cp_nb(x).wait()
        for y in range(8):
            blocks = jnp.concatenate([nb_v[x, y, k] for k in range(9)], axis=1)
            keep = [mask_ref[x, y, k].astype(F32) for k in range(9)]
            source = jnp.concatenate(
                [
                    (epad[x + 1 + dx, y + 1 + dy].astype(F32) * keep[k]).astype(BF16)
                    for k, (dx, dy) in enumerate(NEAR)
                ],
                axis=1,
            )
            nf[x, y] = nt(source, blocks)
            back = nn(wts[x, y], blocks)
            for k, (dx, dy) in enumerate(NEAR):
                acc[x + 1 + dx, y + 1 + dy] += keep[k] * back[:, k * 128 : k * 128 + 128]
        return carry

    lax.fori_loop(0, 2, near, 0)

    for row, present in row_peers():

        @pl.when(present)
        def _():
            l3_row_copy(row, jnp.int32(row)).wait_recv()

    for step in range(3):
        l3_col_start(step)

    lax.fori_loop(2, 4, near, 0)

    l3_col_received(0)

    def up_strip(ref, col, first, rows):
        total = 0.0
        for a in range(2):
            pairs = [
                jnp.concatenate(
                    [
                        ref[col, first + 2 * u + a].reshape(64, 128),
                        ref[col + 1, first + 2 * u + a].reshape(64, 128),
                    ],
                    axis=1,
                )
                for u in range(rows)
            ]
            total = total + nt(jnp.concatenate(pairs, axis=0), ups[a])
        return total.astype(BF16).reshape(rows, 2, 32, 128)

    l4[c2 + 2, pl.ds(2 + part * (c % 2), part)] = up_strip(l3, 2, 2 + 2 * part * (c % 2), part)
    l4_copy(mirror, c2, mirror).start()
    for v in ring:
        l4_copy(v, c2, v).start()

    for number in (2, 3):
        halo_start(number, COL)

    lax.fori_loop(4, 7, near, 0)

    l4_copy(mirror, mirror, mirror).wait_recv()
    for v in ring:
        l4_copy(v, mirror, mirrored(v)).start()
    l3_col_received(1)
    l3_col_start(3)
    l3_col_received(2)
    l3_col_start(4)

    lax.fori_loop(7, 8, near, 0)

    for place, row in ((0, 9), (1, 0)):
        ret_row[place] = acc[row].astype(BF16)
    halo_start(4, ROW)

    halo_received(1, ROW)
    halo_start(1, CORNER)
    ring_rows(leaf, l1, 4, 4)
    halo_received(1, COL)

    INNER, OUTER, COARSE = (1, 2), (0, 3), ()

    def sources(group, side, a, dx, dy):
        parts = []
        for i in group:
            parts.append(leaf[2 * i + a + dx + 2, 1 + dy : 5 + dy, side].reshape(128, 256))
        if group:
            return jnp.concatenate(parts, axis=0)
        for i in range(2):
            parts.append(l1[2 * i + a + dx + 2, 1 + dy : 3 + dy, side].reshape(64, 256))
        parts.append(l2[a + dx + 2, 1 + dy, side])
        for ref, row, col in (
            (l3, 2 * r2, 0),
            (l4, 2 * r4, 2 * c4),
            (l5, 0, 2 * (c // 8)),
        ):
            row = row + a + dx + 2
            col = col + 2 * (1 + dy)
            parts.append(jnp.concatenate([ref[col, row, side], ref[col + 1, row, side]], axis=1))
        return jnp.concatenate(parts, axis=0)

    def interact(group, side, a):
        offsets = [
            (dx, dy)
            for dx in range(-2 - a, 4 - a)
            for dy in (-1, 0, 1)
            if abs(dx) >= 2 or dy != 0
        ]
        total = 0.0
        for dx, dy in offsets:
            taken = sources(group, side, a, dx, dy)
            if side == 0:
                total = total + nt(taken, wt[3 * (dx + 3) + dy + 1])
            else:
                total = total + nn(taken, wt[3 * (3 - dx) + 1 - dy])
        return total

    def inner_rows():
        for side in range(2):
            for a in range(2):
                gain[side, a, 128:384] = interact(INNER, side, a)

    inner_rows()
    for v in ring:
        l4_copy(v, v, v).wait_recv()
        l4_copy(v, mirrored(v), mirrored(v)).wait_recv()

    l4_pass(c % 2).start()
    halo_received(2, ROW)
    halo_start(2, CORNER)
    ring_rows(l1, l2, 2, 2)
    halo_received(3, ROW)
    halo_start(3, CORNER)
    halo_received(1, CORNER)
    for side in range(2):
        for a in range(2):
            made = interact(OUTER, side, a)
            gain[side, a, 0:128] = made[0:128]
            gain[side, a, 384:OFF1] = made[128:256]

    halo_received(4, ROW)
    for place, row in ((0, 1), (1, 8)):
        acc[row] += in_row[place].astype(F32)
    for place, col in ((0, 9), (1, 0)):
        ret_col[place] = acc[1:9, col].astype(BF16)
    halo_start(4, COL)
    l3_col_received(3)
    l3_col_received(4)
    l4_pass(1 - c % 2).wait_recv()
    for col in range(n_cols // 4):
        l5[col + 2, 2 : 2 + n_rows // 4] = up_strip(l4, 2 + 2 * col, 2, n_rows // 4)
    halo_received(2, COL + CORNER)
    ring_cols(leaf, l1, 4, 4)
    ring_cols(l1, l2, 2, 2)
    halo_received(3, COL + CORNER)

    for side in range(2):
        for a in range(2):
            gain[side, a, OFF1:ROWS] = interact(COARSE, side, a)

    for a in range(2):
        for side in range(2):
            top = gain[side, a, OFF5 : OFF5 + 32].astype(BF16)
            for b in range(2):
                sel5[a, b, side] = top[:, b * 128 : b * 128 + 128]
    parent = sel5[r4, c4 % 2].reshape(64, 128)
    for off, sel, row, col in (
        (OFF4, sel4, r2 % 2, c2 % 2),
        (OFF3, sel3, r % 2, c % 2),
        (OFF2, loc2, None, None),
    ):
        for a in range(2):
            spread = nn(parent, ups[a])
            for side in range(2):
                made = spread[side * 32 : side * 32 + 32] + gain[side, a, off : off + 32]
                made = made.astype(BF16)
                for b in range(2):
                    sel[a, b, side] = made[:, b * 128 : b * 128 + 128]
        if row is not None:
            parent = sel[row, col].reshape(64, 128)

    for upper, lower, count, off in ((loc2, loc1, 2, OFF1), (loc1, locl, 4, 0)):
        for u in range(count):
            for a in range(2):
                spread = nn(upper[u].reshape(count * 64, 128), ups[a])
                for v in range(count):
                    for side in range(2):
                        first = v * 64 + side * 32
                        at = off + (u * count + v) * 32
                        made = spread[first : first + 32] + gain[side, a, at : at + 32]
                        made = made.astype(BF16)
                        for b in range(2):
                            lower[2 * u + a, 2 * v + b, side] = made[:, b * 128 : b * 128 + 128]

    halo_received(4, COL)
    for place, col in ((0, 1), (1, 8)):
        acc[1:9, col] += in_col[place].astype(F32)

    def finish(x, carry):
        for y in range(8):
            pot_ref[x, y] = (nf[x, y] + nt(locl[x, y, 0], te_v[x, y])).astype(BF16)
            adj_ref[x, y] = (acc[x + 1, y + 1] + nn(locl[x, y, 1], sm_v[x, y])).astype(BF16)
        return carry

    lax.fori_loop(0, 8, finish, 0)

    for number in range(5):
        halo_sent(number, ROW + COL + (CORNER if number < 4 else []))
    for row, present in row_peers():

        @pl.when(present)
        def _():
            l3_row_copy(row, r).wait_send()

    for step in range(5):

        @pl.when(COL_SENDS[step])
        def _():
            l3_col_copy(step).wait_send()

    l4_pass(c % 2).wait_send()
    l4_copy(mirror, c2, mirror).wait_send()
    for v in ring:
        l4_copy(v, c2, v).wait_send()
        l4_copy(v, mirror, mirrored(v)).wait_send()


def solution(mesh):
    n_rows, n_cols = mesh.shape["bx"], mesh.shape["by"]
    hbm = pl.BlockSpec(memory_space=pl.ANY)
    vmem = pl.BlockSpec(memory_space=pltpu.VMEM)
    box = (2, 32, 128)
    pair = (2, 32, 256)
    scratch = [
        pltpu.VMEM((10, 10, 32, 128), BF16),
        pltpu.VMEM((8, 8, 128), BF16),
        pltpu.VMEM((8, 8, 128), jnp.int32),
        pltpu.VMEM((8, 8, 9, 128, 128), BF16),
        pltpu.VMEM((8, 8, 128, 128), BF16),
        pltpu.VMEM((8, 8, 128, 128), BF16),
        pltpu.VMEM((40, 128, 128), BF16),
        pltpu.VMEM((2, 2, 128, 128), BF16),
        pltpu.VMEM((8, 8, 32, 128), BF16),
        pltpu.VMEM((12, 6) + pair, BF16),
        pltpu.VMEM((8, 4) + pair, BF16),
        pltpu.VMEM((6, 3) + pair, BF16),
        pltpu.VMEM((6, n_rows + 4) + box, BF16),
        pltpu.VMEM((n_cols // 2 + 4, n_rows // 2 + 4) + box, BF16),
        pltpu.VMEM((n_cols // 4 + 4, n_rows // 4 + 4) + box, BF16),
        pltpu.SMEM((8, 8, 9), jnp.int32),
        pltpu.VMEM((8, 8, 32, 128), F32),
        pltpu.VMEM((10, 10, 32, 128), F32),
        pltpu.VMEM((2, 10, 32, 128), BF16),
        pltpu.VMEM((2, 8, 32, 128), BF16),
        pltpu.VMEM((2, 10, 32, 128), BF16),
        pltpu.VMEM((2, 8, 32, 128), BF16),
        pltpu.VMEM((21, 256, 256), BF16),
        pltpu.VMEM((2, 2, ROWS, 256), F32),
        pltpu.VMEM((2, 2) + box, BF16),
        pltpu.VMEM((2, 2) + box, BF16),
        pltpu.VMEM((2, 2) + box, BF16),
        pltpu.VMEM((2, 2) + box, BF16),
        pltpu.VMEM((4, 4) + box, BF16),
        pltpu.VMEM((8, 8) + box, BF16),
        pltpu.SemaphoreType.DMA((6,)),
        pltpu.SemaphoreType.DMA((2, 8)),
        pltpu.SemaphoreType.DMA((8,)),
        pltpu.SemaphoreType.DMA((5, 8)),
        pltpu.SemaphoreType.DMA((5, 8)),
        pltpu.SemaphoreType.DMA((n_rows,)),
        pltpu.SemaphoreType.DMA((n_rows,)),
        pltpu.SemaphoreType.DMA((6,)),
        pltpu.SemaphoreType.DMA((6,)),
        pltpu.SemaphoreType.DMA((n_cols // 2,)),
        pltpu.SemaphoreType.DMA((n_cols // 2,)),
    ]

    def per_device(*arrays):
        def body(*refs):
            kernel(n_rows, n_cols, *refs)

        kept = pltpu.VMEM(arrays[0].shape, BF16)
        return pl.pallas_call(
            body,
            out_shape=(kept, kept),
            in_specs=[hbm, hbm, hbm, hbm, hbm, hbm, hbm, hbm, hbm],
            out_specs=(vmem, vmem),
            scratch_shapes=scratch,
            compiler_params=pltpu.CompilerParams(
                collective_id=0, has_side_effects=True, vmem_limit_bytes=56 * 1024 * 1024
            ),
            cost_estimate=pl.CostEstimate(
                flops=4300000000, bytes_accessed=26000000, transcendentals=0
            ),
            name="fmm",
        )(*arrays)

    placed = (
        P("bx", "by", None, None),
        P("bx", "by", None),
        P("bx", "by", None),
        P("bx", "by", None, None, None),
        P("bx", "by", None),
        P("bx", "by", None, None),
        P("bx", "by", None, None),
        P(),
        P(),
    )
    return jax.shard_map(
        per_device,
        mesh=mesh,
        in_specs=placed,
        out_specs=(P("bx", "by", None, None), P("bx", "by", None, None)),
        check_vma=False,
    )
```

```python
import jax
import jax.numpy as jnp
from jax import lax
from jax.experimental import pallas as pl
from jax.experimental.pallas import tpu as pltpu
from jax.sharding import PartitionSpec as P

MESH = pl.DeviceIdType.MESH
F32 = jnp.float32
BF16 = jnp.bfloat16
DIRS = [(dx, dy) for dx in (-1, 0, 1) for dy in (-1, 0, 1) if (dx, dy) != (0, 0)]
NEAR = [(dx, dy) for dx in (-1, 0, 1) for dy in (-1, 0, 1)]
FAR = [(dx, dy) for dx in range(-3, 4) for dy in range(-3, 4) if max(abs(dx), abs(dy)) >= 2]
OFF1, OFF2, OFF3, OFF4, OFF5, ROWS = 512, 640, 672, 704, 736, 768


def nt(a, b):
    return lax.dot_general(a, b, (((1,), (1,)), ((), ())), preferred_element_type=F32)


def nn(a, b):
    return jnp.dot(a, b, preferred_element_type=F32)


def edge(step, size, width):
    if step == 0:
        return pl.ds(width, size), pl.ds(width, size)
    if step > 0:
        return pl.ds(size, width), pl.ds(0, width)
    return pl.ds(width, width), pl.ds(size + width, width)


def kernel(
    n_rows,
    n_cols,
    exc_hbm,
    area_hbm,
    cond_hbm,
    nb_hbm,
    mask_hbm,
    sm_hbm,
    te_hbm,
    tr_hbm,
    su_hbm,
    pot_ref,
    adj_ref,
    epad,
    area_v,
    cond_v,
    nb_v,
    sm_v,
    te_v,
    tr_v,
    su_v,
    wts,
    leaf,
    l1,
    l2,
    l3,
    l4,
    l5,
    mask_ref,
    nf,
    acc,
    ret_row,
    ret_col,
    in_row,
    in_col,
    wt,
    gain,
    sel5,
    sel4,
    sel3,
    loc2,
    loc1,
    locl,
    in_sem,
    map_sem,
    nb_sem,
    hs_sem,
    hr_sem,
    s3_sem,
    r3_sem,
    sp_sem,
    rp_sem,
    s4_sem,
    r4_sem,
):
    r = lax.axis_index("bx")
    c = lax.axis_index("by")
    r2, c2 = r // 2, c // 2
    r4, c4 = r // 4, c // 4

    cp_exc = pltpu.make_async_copy(exc_hbm, epad.at[1:9, 1:9], in_sem.at[0])
    cp_area = pltpu.make_async_copy(area_hbm, area_v, in_sem.at[1])
    cp_cond = pltpu.make_async_copy(cond_hbm, cond_v, in_sem.at[2])
    cp_su = pltpu.make_async_copy(su_hbm, su_v, in_sem.at[3])
    cp_mask = pltpu.make_async_copy(mask_hbm, mask_ref, in_sem.at[5])
    cp_tr = pltpu.make_async_copy(tr_hbm, tr_v, in_sem.at[4])

    def cp_sm(x):
        return pltpu.make_async_copy(sm_hbm.at[x], sm_v.at[x], map_sem.at[0, x])

    def cp_te(x):
        return pltpu.make_async_copy(te_hbm.at[x], te_v.at[x], map_sem.at[1, x])

    def cp_nb(x):
        return pltpu.make_async_copy(nb_hbm.at[x], nb_v.at[x], nb_sem.at[x])

    cp_exc.start()
    cp_area.start()
    cp_cond.start()
    for x in range(8):
        cp_sm(x).start()
        cp_te(x).start()
    cp_su.start()
    cp_tr.start()
    cp_mask.start()
    for x in range(8):
        cp_nb(x).start()

    def clear(ref, rows, cols, width, wide):
        ref[0:width] = jnp.zeros((width,) + ref.shape[1:], ref.dtype)
        ref[rows + width :] = jnp.zeros((width,) + ref.shape[1:], ref.dtype)
        side = jnp.zeros((rows, wide) + ref.shape[2:], ref.dtype)
        ref[width : rows + width, 0:wide] = side
        ref[width : rows + width, cols + wide :] = side

    clear(epad, 8, 8, 1, 1)
    clear(leaf, 8, 4, 2, 1)
    clear(l1, 4, 2, 2, 1)
    clear(l2, 2, 1, 2, 1)
    for ref in (l3, l4, l5, in_row, in_col):
        ref[...] = jnp.zeros(ref.shape, ref.dtype)

    def inside(row, col):
        return (row >= 0) & (row < n_rows) & (col >= 0) & (col < n_cols)

    def row_peers():
        return [(row, row != r) for row in range(n_rows)]

    def pair_peers():
        return [(v, 2 * v + c % 2, v != c2) for v in range(n_cols // 2)]

    barrier = pltpu.get_barrier_semaphore()
    greeted = jnp.int32(0)

    def greet(row, col, present):
        @pl.when(present)
        def _():
            pl.semaphore_signal(barrier, inc=1, device_id=(row, col), device_id_type=MESH)

        return present.astype(jnp.int32)

    for dy in (-1, 1):
        greeted = greeted + greet(r, c + dy, inside(r, c + dy))
    for row, present in row_peers():
        greeted = greeted + greet(jnp.int32(row), c, present)
    for _, col, present in pair_peers():
        greeted = greeted + greet(r, col, present)
    pl.semaphore_wait(barrier, greeted)

    def halo_copy(number, direction):
        dx, dy = DIRS[direction]
        if number == 4:
            place = 0 if dx + dy > 0 else 1
            src, dst = (ret_row, in_row) if dy == 0 else (ret_col, in_col)
            src, dst = src.at[place], dst.at[place]
        else:
            ref, rows, width, cols, wide = (
                (epad, 8, 1, 8, 1),
                (leaf, 8, 2, 4, 1),
                (l1, 4, 2, 2, 1),
                (l2, 2, 2, 1, 1),
            )[number]
            src_rows, dst_rows = edge(dx, rows, width)
            src_cols, dst_cols = edge(dy, cols, wide)
            if number < 2 or dx * dy != 0:
                src = ref.at[src_rows if dy == 0 or dx == 0 else dst_rows, src_cols]
                dst = ref.at[dst_rows, dst_cols]
            elif dy == 0:
                src = ref.at[rows if dx > 0 else 3, 1 : cols + 1]
                dst = ref.at[0 if dx > 0 else rows + 3, 1 : cols + 1]
            else:
                lanes = slice(0, 128) if dy > 0 else slice(128, 256)
                src = ref.at[src_rows, cols if dy > 0 else 1, :, :, lanes]
                dst = ref.at[dst_rows, 0 if dy > 0 else cols + 1, :, :, lanes]
        return pltpu.make_async_remote_copy(
            src_ref=src,
            dst_ref=dst,
            send_sem=hs_sem.at[number, direction],
            recv_sem=hr_sem.at[number, direction],
            device_id=(r + dx, c) if dy == 0 else (r, c + dy),
            device_id_type=MESH,
        )

    ROW = [i for i, (dx, dy) in enumerate(DIRS) if dy == 0]
    COL = [i for i, (dx, dy) in enumerate(DIRS) if dx == 0]
    CORNER = [i for i, (dx, dy) in enumerate(DIRS) if dx * dy != 0]

    def leaves(direction):
        dx, dy = DIRS[direction]
        if dy == 0:
            return inside(r + dx, c)
        return inside(r - dx, c) & inside(r, c + dy)

    def halo_start(number, directions):
        for direction in directions:

            @pl.when(leaves(direction))
            def _():
                halo_copy(number, direction).start()

    def halo_received(number, directions):
        for direction in directions:
            dx, dy = DIRS[direction]

            @pl.when(inside(r - dx, c - dy))
            def _():
                halo_copy(number, direction).wait_recv()

    def halo_sent(number, directions):
        for direction in directions:

            @pl.when(leaves(direction))
            def _():
                halo_copy(number, direction).wait_send()

    def l3_row_copy(row, sender):
        return pltpu.make_async_remote_copy(
            src_ref=l3.at[2 + c % 2, sender + 2],
            dst_ref=l3.at[2 + c % 2, sender + 2],
            send_sem=s3_sem.at[row],
            recv_sem=r3_sem.at[sender],
            device_id=(jnp.int32(row), c),
            device_id_type=MESH,
        )

    other = c + 1 - 2 * (c % 2)

    def l3_col_copy(step, received=False):
        rows = pl.ds(2, n_rows) if step == 0 else pl.ds(2 * r2, 6)
        own = 2 + c % 2
        there = 2 + (1 - c % 2) if received else own
        if step == 0:
            src, dst, col = own, there, other
        elif step == 1:
            src, dst, col = own, c % 2, c + 2
        elif step == 2:
            src, dst, col = own, 4 + c % 2, c - 2
        else:
            src = c % 2 + (0 if step == 3 else 4)
            dst = (1 - c % 2 if received else c % 2) + (0 if step == 3 else 4)
            col = other
        return pltpu.make_async_remote_copy(
            src_ref=l3.at[src, rows],
            dst_ref=l3.at[dst, rows],
            send_sem=sp_sem.at[step],
            recv_sem=rp_sem.at[step],
            device_id=(r, col),
            device_id_type=MESH,
        )

    has_last, has_next = c2 > 0, c2 < n_cols // 2 - 1
    COL_SENDS = (True, has_next, has_last, has_last, has_next)
    COL_COMES = (True, has_last, has_next, has_last, has_next)

    part = n_rows // 4

    quarter = n_cols // 4
    mirror = (c2 + quarter) % (2 * quarter)
    ring = [quarter * (c2 // quarter) + (c2 + k) % quarter for k in range(1, quarter)]

    def l4_copy(to, owner, slot):
        place = l4.at[owner + 2, pl.ds(2 + part * (c % 2), part)]
        return pltpu.make_async_remote_copy(
            src_ref=place,
            dst_ref=place,
            send_sem=s4_sem.at[slot],
            recv_sem=r4_sem.at[owner],
            device_id=(r, 2 * to + c % 2),
            device_id_type=MESH,
        )

    def mirrored(v):
        return (v + quarter) % (2 * quarter)

    def l4_pass(half):
        place = l4.at[pl.ds(2, n_cols // 2), pl.ds(2 + part * half, part)]
        return pltpu.make_async_remote_copy(
            src_ref=place,
            dst_ref=place,
            send_sem=sp_sem.at[5],
            recv_sem=rp_sem.at[5],
            device_id=(r, other),
            device_id_type=MESH,
        )

    def l3_col_start(step):
        @pl.when(COL_SENDS[step])
        def _():
            l3_col_copy(step).start()

    def l3_col_received(step):
        @pl.when(COL_COMES[step])
        def _():
            l3_col_copy(step, True).wait_recv()

    cp_exc.wait()
    halo_start(0, ROW + COL)
    acc[...] = jnp.zeros(acc.shape, F32)
    cp_area.wait()
    cp_cond.wait()

    labels = lax.broadcasted_iota(jnp.int32, (32, 128), 0)

    def moments(x, carry):
        cp_sm(x).wait()
        cp_te(x).wait()
        conds = cond_v[x]
        areas = area_v[x].astype(F32)
        for y in range(8):
            half = slice((y % 2) * 128, (y % 2) * 128 + 128)
            chosen = labels == conds[y : y + 1]
            w = jnp.where(chosen, areas[y : y + 1], 0.0).astype(BF16)
            wts[x, y] = w
            leaf[x + 2, 1 + y // 2, 0, :, half] = nt(epad[x + 1, y + 1], sm_v[x, y]).astype(BF16)
            leaf[x + 2, 1 + y // 2, 1, :, half] = nn(w, te_v[x, y]).astype(BF16)
        return carry

    lax.fori_loop(0, 8, moments, 0)

    cp_su.wait()
    ups = [jnp.concatenate([su_v[a, 0], su_v[a, 1]], axis=1) for a in range(2)]

    def ring_rows(lower, upper, rows, cols):
        total = sum(
            nt(
                jnp.concatenate(
                    [lower[low + a, 1 : cols + 1].reshape(cols * 64, 256) for low in (0, 2 * rows + 2)],
                    axis=0,
                ),
                ups[a],
            )
            for a in range(2)
        )
        made = total.astype(BF16).reshape(2, cols, 2, 32, 128)
        for place, row in ((0, 1), (1, rows + 2)):
            for v in range(cols):
                upper[row, 1 + v // 2, :, :, (v % 2) * 128 : (v % 2) * 128 + 128] = made[place, v]

    def ring_cols(lower, upper, rows, cols):
        total = sum(
            nt(
                jnp.concatenate(
                    [
                        lower[2 * u + a + 2, col].reshape(64, 256)
                        for col in (0, cols + 1)
                        for u in range(rows)
                    ],
                    axis=0,
                ),
                ups[a],
            )
            for a in range(2)
        )
        made = total.astype(BF16).reshape(2, rows, 2, 32, 128)
        upper[2 : rows + 2, 0, :, :, 128:256] = made[0]
        upper[2 : rows + 2, cols // 2 + 1, :, :, 0:128] = made[1]

    for u in range(4):
        total = sum(nt(leaf[2 * u + a + 2, 1:5].reshape(256, 256), ups[a]) for a in range(2))
        made = total.astype(BF16).reshape(4, 2, 32, 128)
        for v in range(4):
            l1[u + 2, 1 + v // 2, :, :, (v % 2) * 128 : (v % 2) * 128 + 128] = made[v]
    total = sum(
        nt(jnp.concatenate([l1[2 * u + a + 2, 1:3].reshape(128, 256) for u in range(2)]), ups[a])
        for a in range(2)
    )
    made = total.astype(BF16).reshape(2, 2, 2, 32, 128)
    for u in range(2):
        for v in range(2):
            l2[u + 2, 1, :, :, v * 128 : v * 128 + 128] = made[u, v]
    total = sum(nt(l2[a + 2, 1].reshape(64, 256), ups[a]) for a in range(2))
    l3[2 + c % 2, r + 2] = total.astype(BF16).reshape(2, 32, 128)

    for row, present in row_peers():

        @pl.when(present)
        def _():
            l3_row_copy(row, r).start()

    for number in (1, 2, 3):
        halo_start(number, ROW)
    halo_received(0, ROW)
    halo_start(0, CORNER)
    for number in (1,):
        halo_start(number, COL)

    cp_tr.wait()
    for dx in range(-3, 4):
        for dy in range(-1, 2):
            for i in range(2):
                for j in range(2):
                    offset = (dx, 2 * dy + j - i)
                    block = (
                        tr_v[FAR.index(offset)] if offset in FAR else jnp.zeros((128, 128), BF16)
                    )
                    wt[
                        3 * (dx + 3) + dy + 1,
                        i * 128 : i * 128 + 128,
                        j * 128 : j * 128 + 128,
                    ] = block

    halo_received(0, COL + CORNER)
    cp_mask.wait()

    def near(x, carry):
        cp_nb(x).wait()
        for y in range(8):
            blocks = jnp.concatenate([nb_v[x, y, k] for k in range(9)], axis=1)
            keep = [mask_ref[x, y, k].astype(F32) for k in range(9)]
            source = jnp.concatenate(
                [
                    (epad[x + 1 + dx, y + 1 + dy].astype(F32) * keep[k]).astype(BF16)
                    for k, (dx, dy) in enumerate(NEAR)
                ],
                axis=1,
            )
            nf[x, y] = nt(source, blocks)
            back = nn(wts[x, y], blocks)
            for k, (dx, dy) in enumerate(NEAR):
                acc[x + 1 + dx, y + 1 + dy] += keep[k] * back[:, k * 128 : k * 128 + 128]
        return carry

    lax.fori_loop(0, 2, near, 0)

    for row, present in row_peers():

        @pl.when(present)
        def _():
            l3_row_copy(row, jnp.int32(row)).wait_recv()

    for step in range(3):
        l3_col_start(step)

    lax.fori_loop(2, 4, near, 0)

    l3_col_received(0)

    def up_strip(ref, col, first, rows):
        total = 0.0
        for a in range(2):
            pairs = [
                jnp.concatenate(
                    [
                        ref[col, first + 2 * u + a].reshape(64, 128),
                        ref[col + 1, first + 2 * u + a].reshape(64, 128),
                    ],
                    axis=1,
                )
                for u in range(rows)
            ]
            total = total + nt(jnp.concatenate(pairs, axis=0), ups[a])
        return total.astype(BF16).reshape(rows, 2, 32, 128)

    l4[c2 + 2, pl.ds(2 + part * (c % 2), part)] = up_strip(l3, 2, 2 + 2 * part * (c % 2), part)
    l4_copy(mirror, c2, mirror).start()
    for v in ring:
        l4_copy(v, c2, v).start()

    for number in (2, 3):
        halo_start(number, COL)

    lax.fori_loop(4, 7, near, 0)

    l4_copy(mirror, mirror, mirror).wait_recv()
    for v in ring:
        l4_copy(v, mirror, mirrored(v)).start()
    l3_col_received(1)
    l3_col_start(3)
    l3_col_received(2)
    l3_col_start(4)

    lax.fori_loop(7, 8, near, 0)

    for place, row in ((0, 9), (1, 0)):
        ret_row[place] = acc[row].astype(BF16)
    halo_start(4, ROW)

    halo_received(1, ROW)
    halo_start(1, CORNER)
    ring_rows(leaf, l1, 4, 4)
    halo_received(2, ROW)
    halo_start(2, CORNER)
    ring_rows(l1, l2, 2, 2)
    halo_received(3, ROW)
    halo_start(3, CORNER)
    halo_received(1, COL)

    INNER, OUTER, COARSE = (1, 2), (0, 3), ()

    def sources(group, side, a, dx, dy):
        parts = []
        for i in group:
            parts.append(leaf[2 * i + a + dx + 2, 1 + dy : 5 + dy, side].reshape(128, 256))
        if group:
            return jnp.concatenate(parts, axis=0)
        for i in range(2):
            parts.append(l1[2 * i + a + dx + 2, 1 + dy : 3 + dy, side].reshape(64, 256))
        parts.append(l2[a + dx + 2, 1 + dy, side])
        for ref, row, col in (
            (l3, 2 * r2, 0),
            (l4, 2 * r4, 2 * c4),
            (l5, 0, 2 * (c // 8)),
        ):
            row = row + a + dx + 2
            col = col + 2 * (1 + dy)
            parts.append(jnp.concatenate([ref[col, row, side], ref[col + 1, row, side]], axis=1))
        return jnp.concatenate(parts, axis=0)

    def interact(group, side, a):
        offsets = [
            (dx, dy)
            for dx in range(-2 - a, 4 - a)
            for dy in (-1, 0, 1)
            if abs(dx) >= 2 or dy != 0
        ]
        total = 0.0
        for dx, dy in offsets:
            taken = sources(group, side, a, dx, dy)
            if side == 0:
                total = total + nt(taken, wt[3 * (dx + 3) + dy + 1])
            else:
                total = total + nn(taken, wt[3 * (3 - dx) + 1 - dy])
        return total

    def inner_rows():
        for side in range(2):
            for a in range(2):
                gain[side, a, 128:384] = interact(INNER, side, a)

    inner_rows()
    for v in ring:
        l4_copy(v, v, v).wait_recv()
        l4_copy(v, mirrored(v), mirrored(v)).wait_recv()

    l4_pass(c % 2).start()
    halo_received(1, CORNER)
    for side in range(2):
        for a in range(2):
            made = interact(OUTER, side, a)
            gain[side, a, 0:128] = made[0:128]
            gain[side, a, 384:OFF1] = made[128:256]

    halo_received(4, ROW)
    for place, row in ((0, 1), (1, 8)):
        acc[row] += in_row[place].astype(F32)
    for place, col in ((0, 9), (1, 0)):
        ret_col[place] = acc[1:9, col].astype(BF16)
    halo_start(4, COL)
    l3_col_received(3)
    l3_col_received(4)
    l4_pass(1 - c % 2).wait_recv()
    for col in range(n_cols // 4):
        l5[col + 2, 2 : 2 + n_rows // 4] = up_strip(l4, 2 + 2 * col, 2, n_rows // 4)
    halo_received(2, COL + CORNER)
    ring_cols(leaf, l1, 4, 4)
    ring_cols(l1, l2, 2, 2)
    halo_received(3, COL + CORNER)

    for side in range(2):
        for a in range(2):
            gain[side, a, OFF1:ROWS] = interact(COARSE, side, a)

    for a in range(2):
        for side in range(2):
            top = gain[side, a, OFF5 : OFF5 + 32].astype(BF16)
            for b in range(2):
                sel5[a, b, side] = top[:, b * 128 : b * 128 + 128]
    parent = sel5[r4, c4 % 2].reshape(64, 128)
    for off, sel, row, col in (
        (OFF4, sel4, r2 % 2, c2 % 2),
        (OFF3, sel3, r % 2, c % 2),
        (OFF2, loc2, None, None),
    ):
        for a in range(2):
            spread = nn(parent, ups[a])
            for side in range(2):
                made = spread[side * 32 : side * 32 + 32] + gain[side, a, off : off + 32]
                made = made.astype(BF16)
                for b in range(2):
                    sel[a, b, side] = made[:, b * 128 : b * 128 + 128]
        if row is not None:
            parent = sel[row, col].reshape(64, 128)

    for upper, lower, count, off in ((loc2, loc1, 2, OFF1), (loc1, locl, 4, 0)):
        for u in range(count):
            for a in range(2):
                spread = nn(upper[u].reshape(count * 64, 128), ups[a])
                for v in range(count):
                    for side in range(2):
                        first = v * 64 + side * 32
                        at = off + (u * count + v) * 32
                        made = spread[first : first + 32] + gain[side, a, at : at + 32]
                        made = made.astype(BF16)
                        for b in range(2):
                            lower[2 * u + a, 2 * v + b, side] = made[:, b * 128 : b * 128 + 128]

    halo_received(4, COL)
    for place, col in ((0, 1), (1, 8)):
        acc[1:9, col] += in_col[place].astype(F32)

    def finish(x, carry):
        for y in range(8):
            pot_ref[x, y] = (nf[x, y] + nt(locl[x, y, 0], te_v[x, y])).astype(BF16)
            adj_ref[x, y] = (acc[x + 1, y + 1] + nn(locl[x, y, 1], sm_v[x, y])).astype(BF16)
        return carry

    lax.fori_loop(0, 8, finish, 0)

    for number in range(5):
        halo_sent(number, ROW + COL + (CORNER if number < 4 else []))
    for row, present in row_peers():

        @pl.when(present)
        def _():
            l3_row_copy(row, r).wait_send()

    for step in range(5):

        @pl.when(COL_SENDS[step])
        def _():
            l3_col_copy(step).wait_send()

    l4_pass(c % 2).wait_send()
    l4_copy(mirror, c2, mirror).wait_send()
    for v in ring:
        l4_copy(v, c2, v).wait_send()
        l4_copy(v, mirror, mirrored(v)).wait_send()


def solution(mesh):
    n_rows, n_cols = mesh.shape["bx"], mesh.shape["by"]
    hbm = pl.BlockSpec(memory_space=pl.ANY)
    vmem = pl.BlockSpec(memory_space=pltpu.VMEM)
    box = (2, 32, 128)
    pair = (2, 32, 256)
    scratch = [
        pltpu.VMEM((10, 10, 32, 128), BF16),
        pltpu.VMEM((8, 8, 128), BF16),
        pltpu.VMEM((8, 8, 128), jnp.int32),
        pltpu.VMEM((8, 8, 9, 128, 128), BF16),
        pltpu.VMEM((8, 8, 128, 128), BF16),
        pltpu.VMEM((8, 8, 128, 128), BF16),
        pltpu.VMEM((40, 128, 128), BF16),
        pltpu.VMEM((2, 2, 128, 128), BF16),
        pltpu.VMEM((8, 8, 32, 128), BF16),
        pltpu.VMEM((12, 6) + pair, BF16),
        pltpu.VMEM((8, 4) + pair, BF16),
        pltpu.VMEM((6, 3) + pair, BF16),
        pltpu.VMEM((6, n_rows + 4) + box, BF16),
        pltpu.VMEM((n_cols // 2 + 4, n_rows // 2 + 4) + box, BF16),
        pltpu.VMEM((n_cols // 4 + 4, n_rows // 4 + 4) + box, BF16),
        pltpu.SMEM((8, 8, 9), jnp.int32),
        pltpu.VMEM((8, 8, 32, 128), F32),
        pltpu.VMEM((10, 10, 32, 128), F32),
        pltpu.VMEM((2, 10, 32, 128), BF16),
        pltpu.VMEM((2, 8, 32, 128), BF16),
        pltpu.VMEM((2, 10, 32, 128), BF16),
        pltpu.VMEM((2, 8, 32, 128), BF16),
        pltpu.VMEM((21, 256, 256), BF16),
        pltpu.VMEM((2, 2, ROWS, 256), F32),
        pltpu.VMEM((2, 2) + box, BF16),
        pltpu.VMEM((2, 2) + box, BF16),
        pltpu.VMEM((2, 2) + box, BF16),
        pltpu.VMEM((2, 2) + box, BF16),
        pltpu.VMEM((4, 4) + box, BF16),
        pltpu.VMEM((8, 8) + box, BF16),
        pltpu.SemaphoreType.DMA((6,)),
        pltpu.SemaphoreType.DMA((2, 8)),
        pltpu.SemaphoreType.DMA((8,)),
        pltpu.SemaphoreType.DMA((5, 8)),
        pltpu.SemaphoreType.DMA((5, 8)),
        pltpu.SemaphoreType.DMA((n_rows,)),
        pltpu.SemaphoreType.DMA((n_rows,)),
        pltpu.SemaphoreType.DMA((6,)),
        pltpu.SemaphoreType.DMA((6,)),
        pltpu.SemaphoreType.DMA((n_cols // 2,)),
        pltpu.SemaphoreType.DMA((n_cols // 2,)),
    ]

    def per_device(*arrays):
        def body(*refs):
            kernel(n_rows, n_cols, *refs)

        kept = pltpu.VMEM(arrays[0].shape, BF16)
        return pl.pallas_call(
            body,
            out_shape=(kept, kept),
            in_specs=[hbm, hbm, hbm, hbm, hbm, hbm, hbm, hbm, hbm],
            out_specs=(vmem, vmem),
            scratch_shapes=scratch,
            compiler_params=pltpu.CompilerParams(
                collective_id=0, has_side_effects=True, vmem_limit_bytes=56 * 1024 * 1024
            ),
            cost_estimate=pl.CostEstimate(
                flops=4300000000, bytes_accessed=26000000, transcendentals=0
            ),
            name="fmm",
        )(*arrays)

    placed = (
        P("bx", "by", None, None),
        P("bx", "by", None),
        P("bx", "by", None),
        P("bx", "by", None, None, None),
        P("bx", "by", None),
        P("bx", "by", None, None),
        P("bx", "by", None, None),
        P(),
        P(),
    )
    return jax.shard_map(
        per_device,
        mesh=mesh,
        in_specs=placed,
        out_specs=(P("bx", "by", None, None), P("bx", "by", None, None)),
        check_vma=False,
    )
```
